128 devices in a mesh: fsdp: 32 (over z, y, core), sp: 4 (over x).
Axes of the slice: x: 4, y: 4, z: 4, core: 2. Of those that a mesh axis runs over, the one named last changes fastest.
Arguments:
- hidden_in: bfloat16 [32, 1024, 768], P('fsdp', 'sp'), may hold values from -6 to 6
- lengths: int32 [32], P('fsdp'), may hold values from 128 to 1024, as said below
- qkv_weight: bfloat16 [768, 2304], P('fsdp'), may hold values from -0.21875 to 0.21875
- query_bias: bfloat16 [768], P('fsdp'), may hold values from -3 to 3
- value_bias: bfloat16 [768], P('fsdp'), may hold values from -3 to 3
- context_weight: bfloat16 [768, 768], P('fsdp'), may hold values from -6 to 6
- context_bias: bfloat16 [768], P('fsdp'), may hold values from -3 to 3
- first_gain: bfloat16 [768], P('fsdp'), may hold values from 0.25 to 1.75
- first_shift: bfloat16 [768], P('fsdp'), may hold values from -3 to 3
- expand_weight: bfloat16 [768, 3072], P('fsdp'), may hold values from -0.21875 to 0.21875
- expand_bias: bfloat16 [3072], P('fsdp'), may hold values from -3 to 3
- reduce_weight: bfloat16 [3072, 768], P('fsdp'), may hold values from -0.109375 to 0.109375
- reduce_bias: bfloat16 [768], P('fsdp'), may hold values from -3 to 3
- second_gain: bfloat16 [768], P('fsdp'), may hold values from 0.25 to 1.75
- second_shift: bfloat16 [768], P('fsdp'), may hold values from -3 to 3
- out_grad: bfloat16 [32, 1024, 768], P('fsdp', 'sp'), may hold values from -6 to 6
Outputs:
- hidden_out: bfloat16 [32, 1024, 768], P('fsdp', 'sp')
- input_grad: bfloat16 [32, 1024, 768], P('fsdp', 'sp')
- qkv_weight_grad: float32 [768, 2304], P('fsdp')
- query_bias_grad: float32 [768], P('fsdp')
- value_bias_grad: float32 [768], P('fsdp')
- context_weight_grad: float32 [768, 768], P('fsdp')
- context_bias_grad: float32 [768], P('fsdp')
- first_gain_grad: float32 [768], P('fsdp')
- first_shift_grad: float32 [768], P('fsdp')
- expand_weight_grad: float32 [768, 3072], P('fsdp')
- expand_bias_grad: float32 [3072], P('fsdp')
- reduce_weight_grad: float32 [3072, 768], P('fsdp')
- reduce_bias_grad: float32 [768], P('fsdp')
- second_gain_grad: float32 [768], P('fsdp')
- second_shift_grad: float32 [768], P('fsdp')
The draws below stay inside these ranges and needn't reach their ends.
Inputs may be any that keep to these rules, and one draw needn't show every extreme that they name: lengths of a sequence counts its valid positions from its start; later positions are padding. In every group of 1 sequence one has more than 768, and some sequence has exactly 1024.
All inputs are finite; a program needn't handle non-finite values.
Results may differ from the reference program's by a relative error of at most 0.025.
Values may be sent and summed in bfloat16 or wider, within the bound.
No kernel may reach another device: no remote copies, remote signals or barrier semaphores. Data moves between devices by JAX's collectives and lax.ppermute only.
A program may use at most 128 MiB of HBM per device.

```python
import jax
import jax.numpy as jnp
from jax import lax

D = 768
H = 12
DH = 64
FF = 3072
LEN = 1024
SEQ_DEV = 1
SEQS = 32


def draw_lengths(key, part):
    groups = SEQS // SEQ_DEV
    spread = jax.random.randint(jax.random.fold_in(key, 101), (SEQS,), LEN // 8, LEN + 1)
    longer = jax.random.randint(jax.random.fold_in(key, 102), (SEQS,), 3 * LEN // 4 + 1, LEN + 1)
    chosen = jax.random.randint(jax.random.fold_in(key, 103), (groups,), 0, SEQ_DEV)
    position = jnp.arange(SEQS, dtype=jnp.int32)
    picked = position % SEQ_DEV == jnp.repeat(chosen, SEQ_DEV)
    widest = jax.random.randint(jax.random.fold_in(key, 104), (), 0, SEQS)
    result = jnp.where(picked, longer, spread)
    return jnp.where(position == widest, LEN, result).astype(jnp.int32)


def block_scale(rng, dims, cuts, low, top_value):
    loudness = 1.0
    for axis_at, blocks in cuts:
        draws = jax.random.uniform(jax.random.fold_in(jax.random.fold_in(rng, 6), axis_at), (blocks,), jnp.float32, low / len(cuts), top_value / len(cuts))
        loudness = loudness * jnp.repeat(jnp.exp(draws), dims[axis_at] // blocks).reshape((-1,) + (1,) * (len(dims) - 1 - axis_at))
    return loudness


def bell_draw(stream_key, extent, width, bound, cuts=(), kind=jnp.bfloat16):
    entries = jax.random.normal(stream_key, extent, jnp.float32) * width
    if len(cuts) > 0:
        entries = block_scale(stream_key, extent, cuts, -0.22, 0.18) * entries
    return jnp.clip(entries, min=-bound, max=bound).astype(kind)


def setup_inputs(seed: int = 0) -> dict:
    key_of = jax.random.split(jax.random.key(seed), 17)
    return {
        "hidden_in": bell_draw(key_of[0], (SEQS, LEN, D), 1.0, 6.0, ((0, 32), (1, 4))),
        "lengths": draw_lengths(jax.random.fold_in(key_of[16], 71), 0),
        "qkv_weight": bell_draw(key_of[2], (D, 3 * D), D ** -0.5, 0.21875, ((0, 32),)),
        "query_bias": bell_draw(key_of[3], (D,), 0.5, 3.0, ((0, 32),)),
        "value_bias": bell_draw(key_of[4], (D,), 0.5, 3.0, ((0, 32),)),
        "context_weight": bell_draw(key_of[5], (D, D), (max(1, 2 * D // LEN)) ** -0.5, 6.0, ((0, 32),)),
        "context_bias": bell_draw(key_of[6], (D,), 0.5, 3.0, ((0, 32),)),
        "first_gain": jnp.clip(1.0 + 0.15 * jax.random.normal(key_of[7], (D,), jnp.float32), 0.25, 1.75).astype(jnp.bfloat16),
        "first_shift": bell_draw(key_of[8], (D,), 0.5, 3.0, ((0, 32),)),
        "expand_weight": bell_draw(key_of[9], (D, FF), D ** -0.5, 0.21875, ((0, 32),)),
        "expand_bias": bell_draw(key_of[10], (FF,), 0.5, 3.0, ((0, 32),)),
        "reduce_weight": bell_draw(key_of[11], (FF, D), FF ** -0.5, 0.109375, ((0, 32),)),
        "reduce_bias": bell_draw(key_of[12], (D,), 0.5, 3.0, ((0, 32),)),
        "second_gain": jnp.clip(1.0 + 0.15 * jax.random.normal(key_of[13], (D,), jnp.float32), 0.25, 1.75).astype(jnp.bfloat16),
        "second_shift": bell_draw(key_of[14], (D,), 0.5, 3.0, ((0, 32),)),
        "out_grad": bell_draw(key_of[15], (SEQS, LEN, D), 1.0, 6.0, ((0, 32), (1, 4))),
    }


@jax.custom_vjp
def low(v):
    return lax.optimization_barrier(v.astype(jnp.bfloat16)).astype(jnp.float32)

@jax.custom_vjp
def low_back(v):
    return v

def low_keep(v):
    return (low(v), None)

def low_pass(kept, grad):
    return (grad,)

def back_keep(v):
    return (v, None)

def back_low(kept, grad):
    return (low(grad),)
low.defvjp(low_keep, low_pass)
low_back.defvjp(back_keep, back_low)
EPSILON = 1e-06
SCALING = 0.125
MASKED = -1000000000.0
HIGHEST = lax.Precision.HIGHEST

def product(left_side, right_side):
    return jnp.dot(left_side, right_side, precision=HIGHEST)

def normalize(values, gain_row, shift_row):
    average = lax.optimization_barrier(jnp.mean(values, axis=-1, keepdims=True))
    centred = values - average
    spread = lax.optimization_barrier(jnp.mean(centred * centred, axis=-1, keepdims=True))
    return centred * lax.rsqrt(spread + EPSILON) * gain_row + shift_row

def forward(params, sequence, length):
    qkv_weight, query_bias, value_bias, context_weight, context_bias, first_gain, first_shift, expand_weight, expand_bias, reduce_weight, reduce_bias, second_gain, second_shift = params
    projected = product(sequence, qkv_weight)
    queries = low_back(low(projected[:, :D] + query_bias)).reshape(LEN, H, DH)
    key_heads = low_back(low(projected[:, D:2 * D])).reshape(LEN, H, DH)
    value_heads = low_back(low(projected[:, 2 * D:] + value_bias)).reshape(LEN, H, DH)
    scores = jnp.einsum('qhd,khd->hqk', queries, key_heads, precision=HIGHEST) * SCALING
    key_valid = jnp.arange(LEN) < length
    scores = low_back(jnp.where(key_valid[None, None, :], scores, MASKED))
    probabilities = jax.nn.softmax(scores, axis=-1)
    context = jnp.einsum('hqk,khd->qhd', low(probabilities), value_heads, precision=HIGHEST)
    context = low_back(low(context.reshape(LEN, D)))
    branch = low_back(product(context, context_weight) + context_bias)
    first_out = normalize(sequence + branch, first_gain, first_shift)
    expand = low_back(product(low(first_out), expand_weight) + expand_bias)
    active = low_back(low(jax.nn.gelu(expand, approximate=True)))
    reduced = low_back(product(active, reduce_weight) + reduce_bias)
    return normalize(first_out + reduced, second_gain, second_shift)

def reference(hidden_in, lengths, qkv_weight, query_bias, value_bias, context_weight, context_bias, first_gain, first_shift, expand_weight, expand_bias, reduce_weight, reduce_bias, second_gain, second_shift, out_grad):
    params = tuple((weight_arg.astype(jnp.float32) for weight_arg in (qkv_weight, query_bias, value_bias, context_weight, context_bias, first_gain, first_shift, expand_weight, expand_bias, reduce_weight, reduce_bias, second_gain, second_shift)))

    def one_sequence(grad_total, pieces):
        sequence, length, cotangent = pieces
        result, pullback = jax.vjp(lambda weights, inputs: forward(weights, inputs, length), params, sequence.astype(jnp.float32))
        param_grads, seq_grad = pullback(cotangent.astype(jnp.float32))
        grad_total = jax.tree.map(jnp.add, grad_total, param_grads)
        return (grad_total, (result.astype(jnp.bfloat16), seq_grad.astype(jnp.bfloat16)))
    start_sum = tuple((jnp.zeros(weight_arg.shape, jnp.float32) for weight_arg in params))
    grad_total, (outputs, input_grads) = lax.scan(one_sequence, start_sum, (hidden_in, lengths, out_grad))
    return (outputs, input_grads, grad_total[0], grad_total[1], grad_total[2], grad_total[3], grad_total[4], grad_total[5], grad_total[6], grad_total[7], grad_total[8], grad_total[9], grad_total[10], grad_total[11], grad_total[12])
```

```python
import functools

import jax
import jax.numpy as jnp
from jax import lax
from jax.experimental import pallas as pl
from jax.experimental.pallas import tpu as pltpu
from jax.sharding import PartitionSpec as P

D = 768
H = 12
DH = 64
FF = 3072
SP = 4
LOCAL = 256
LEN = 1024
HEADS = H // SP
HW = HEADS * DH
BLOCK = 256

EPSILON = 1e-06
SCALING = 0.125
MASKED = -1000000000.0
F32 = jnp.float32
BF16 = jnp.bfloat16


def normalize(values, gain_row, shift_row):
    average = jnp.mean(values, axis=-1, keepdims=True)
    centred = values - average
    inv_std = lax.rsqrt(jnp.mean(centred * centred, axis=-1, keepdims=True) + EPSILON)
    normed = centred * inv_std
    return (normed * gain_row + shift_row, normed, inv_std)


def normalize_back(upstream, normed, inv_std, gain_row):
    weighted = upstream * gain_row
    return inv_std * (
        weighted
        - jnp.mean(weighted, axis=-1, keepdims=True)
        - normed * jnp.mean(weighted * normed, axis=-1, keepdims=True)
    )


def dot(left_side, right_side):
    return jnp.dot(left_side, right_side, preferred_element_type=F32)


def rows_first(left_side, right_side):
    return lax.dot_general(
        left_side, right_side, (((0,), (0,)), ((), ())), preferred_element_type=F32
    )


def by_transpose(left_side, right_side):
    return lax.dot_general(
        left_side, right_side, (((1,), (1,)), ((), ())), preferred_element_type=F32
    )


def smooth_gate(values):
    return jax.nn.gelu(values, approximate=True)


def column_sum(values):
    return jnp.sum(values.astype(F32), axis=0)


def to_x(values, step):
    return lax.ppermute(values, "sp", [(i, (i + step) % SP) for i in range(SP)])


def to_y(values, step):
    return lax.ppermute(
        values, "fsdp", [(i, i // 8 * 8 + (i % 8 + 2 * step) % 8) for i in range(32)]
    )


def to_z(values, step):
    return lax.ppermute(values, "fsdp", [(i, (i + 8 * step) % 32) for i in range(32)])


def to_core(values):
    return lax.ppermute(values, "fsdp", [(i, i ^ 1) for i in range(32)])


ORDER = (1, 3, 2)


def pick(values, index, axis=0):
    return lax.dynamic_index_in_dim(values, index, axis, keepdims=False)


def rolled(values, start):
    count = values.shape[0]
    return lax.dynamic_slice_in_dim(
        jnp.concatenate([values, values], axis=0), start % count, count, axis=0
    )


def masked_keys(info_ref, shape, dim):
    at = lax.broadcasted_iota(jnp.int32, shape, dim)
    block = (info_ref[0] + lax.shift_right_logical(at, 8)) & 3
    return (block * LOCAL + (at & (LOCAL - 1))) < info_ref[1]


def attend_kernel(info_ref, qkv_ref, context_ref):
    valid = masked_keys(info_ref, (1, LEN), 1)
    for head in range(HEADS):
        cols = head * DH
        keys = qkv_ref[:, HW + cols : HW + cols + DH]
        vals = qkv_ref[:, 2 * HW + cols : 2 * HW + cols + DH]

        @pl.loop(0, LEN // BLOCK)
        def _(step, keys=keys, vals=vals, cols=cols):
            rows = pl.ds(pl.multiple_of(step * BLOCK, BLOCK), BLOCK)
            queries = qkv_ref[rows, cols : cols + DH] * jnp.asarray(SCALING, BF16)
            scores = jnp.where(valid, by_transpose(queries, keys), MASKED)
            weights = jnp.exp(scores - jnp.max(scores, axis=-1, keepdims=True))
            totals = jnp.sum(weights, axis=-1, keepdims=True)
            low = (weights * (1.0 / totals)).astype(BF16)
            context_ref[rows, cols : cols + DH] = dot(low, vals).astype(BF16)


def attend_back_kernel(info_ref, qkv_ref, grad_ref, out_ref, key_sum, value_sum):
    valid = masked_keys(info_ref, (LEN, 1), 0)
    for head in range(HEADS):
        cols = head * DH
        keys = qkv_ref[:, HW + cols : HW + cols + DH]
        vals = qkv_ref[:, 2 * HW + cols : 2 * HW + cols + DH]
        key_sum[...] = jnp.zeros_like(key_sum)
        value_sum[...] = jnp.zeros_like(value_sum)

        @pl.loop(0, LEN // BLOCK)
        def _(step, keys=keys, vals=vals, cols=cols):
            rows = pl.ds(pl.multiple_of(step * BLOCK, BLOCK), BLOCK)
            queries = qkv_ref[rows, cols : cols + DH] * jnp.asarray(SCALING, BF16)
            grads = grad_ref[rows, cols : cols + DH]
            scores = jnp.where(valid, by_transpose(keys, queries), MASKED)
            weights = jnp.exp(scores - jnp.max(scores, axis=0, keepdims=True))
            probs = weights * (1.0 / jnp.sum(weights, axis=0, keepdims=True))
            value_sum[...] += dot(probs.astype(BF16), grads)
            prob_grad = by_transpose(vals, grads)
            centre = jnp.sum(probs * prob_grad, axis=0, keepdims=True)
            score_grad = (probs * (prob_grad - centre)).astype(BF16)
            key_sum[...] += dot(score_grad, queries)
            out_ref[rows, cols : cols + DH] = (rows_first(score_grad, keys) * SCALING).astype(BF16)

        out_ref[:, HW + cols : HW + cols + DH] = key_sum[...].astype(BF16)
        out_ref[:, 2 * HW + cols : 2 * HW + cols + DH] = value_sum[...].astype(BF16)


SMEM = pl.BlockSpec(memory_space=pltpu.SMEM)
VMEM = pl.BlockSpec(memory_space=pltpu.VMEM)
PARAMS = pltpu.CompilerParams(vmem_limit_bytes=40 * 1024 * 1024)


def attend(info, qkv):
    return pl.pallas_call(
        attend_kernel,
        out_shape=jax.ShapeDtypeStruct((LEN, HW), BF16),
        in_specs=[SMEM, VMEM],
        out_specs=VMEM,
        compiler_params=PARAMS,
        cost_estimate=pl.CostEstimate(
            flops=4 * HEADS * LEN * LEN * 256, bytes_accessed=LEN * HW * 8, transcendentals=0
        ),
        name="attend",
    )(info, qkv)


def attend_back(info, qkv, grads):
    return pl.pallas_call(
        attend_back_kernel,
        out_shape=jax.ShapeDtypeStruct((LEN, 3 * HW), BF16),
        in_specs=[SMEM, VMEM, VMEM],
        out_specs=VMEM,
        scratch_shapes=[pltpu.VMEM((LEN, DH), F32), pltpu.VMEM((LEN, DH), F32)],
        compiler_params=PARAMS,
        cost_estimate=pl.CostEstimate(
            flops=10 * HEADS * LEN * LEN * 256, bytes_accessed=LEN * HW * 14, transcendentals=0
        ),
        name="attend_back",
    )(info, qkv, grads)


def core_sum(values, core):
    other = to_core(pick(values, 1 - core))
    return pick(values, core).astype(F32) + other.astype(F32)


def ring_sum(values, at, send):
    total = pick(values, at).astype(F32)
    for step in ORDER:
        total = total + send(pick(values, (at + step) % 4), step).astype(F32)
    return total


def plane_sum(values, z_at, y_at):
    total = ring_sum(jnp.swapaxes(values, 0, 1), y_at, to_y).astype(BF16)
    return ring_sum(total, z_at, to_z)


def from_x(values, x_at):
    pieces = [values] + [to_x(values, -step) for step in (1, 2, 3)]
    return rolled(jnp.stack(pieces), SP - x_at)


def per_device(
    hidden_in,
    lengths,
    qkv_weight,
    query_bias,
    value_bias,
    context_weight,
    context_bias,
    first_gain,
    first_shift,
    expand_weight,
    expand_bias,
    reduce_weight,
    reduce_bias,
    second_gain,
    second_shift,
    out_grad,
):
    x_at = lax.axis_index("sp")
    fsdp_at = lax.axis_index("fsdp")
    core = fsdp_at % 2
    y_at = fsdp_at // 2 % 4
    z_at = fsdp_at // 8
    own = hidden_in[0]
    tokens = [own] + [None] * 3
    for step in ORDER:
        tokens[step] = to_x(own, -step)

    packed = jnp.concatenate(
        [context_weight, reduce_weight]
        + [expand_weight[:, D * block : D * (block + 1)] for block in range(4)],
        axis=0,
    )
    packed = lax.all_gather(packed, "fsdp", axis=0, tiled=False)

    vectors = jnp.stack(
        [query_bias, value_bias, context_bias, first_gain, first_shift, reduce_bias, second_gain, second_shift],
        axis=1,
    )
    qkv_own = pick(qkv_weight.reshape(24, 3, SP, HW), x_at, 2).reshape(24, 3 * HW)
    early = jnp.concatenate([qkv_own, vectors, expand_bias.reshape(24, 4)], axis=1)
    early = lax.all_to_all(
        jnp.broadcast_to(early[None], (32,) + early.shape).reshape(D, -1),
        "fsdp",
        split_axis=0,
        concat_axis=0,
        tiled=True,
    )
    qkv_full = early[:, : 3 * HW]
    rows = early[:, 3 * HW : 3 * HW + 8].astype(F32).T
    expand_add = early[:, 3 * HW + 8 :].astype(F32).reshape(FF)
    query_full, value_full, context_add, gain_one, shift_one, reduce_add, gain_two, shift_two = rows

    everyone = jnp.concatenate(tokens, axis=0)
    offsets = jnp.concatenate(
        [
            lax.dynamic_slice_in_dim(query_full, x_at * HW, HW),
            jnp.zeros((HW,), F32),
            lax.dynamic_slice_in_dim(value_full, x_at * HW, HW),
        ]
    )
    qkv = (dot(everyone, qkv_full) + offsets).astype(BF16)
    info = jnp.stack([x_at.astype(jnp.int32), lengths[0]])
    context = attend(info, qkv)

    groups = [context[:LOCAL]] + [None] * 3
    for step in ORDER:
        groups[SP - step] = to_x(context[step * LOCAL : (step + 1) * LOCAL], step)
    context_tok = jnp.concatenate(groups, axis=1)

    context_full = rolled(packed[:, :24].reshape(SP, HW, D), x_at).reshape(D, D)
    reduce_full = packed[:, 24:120].reshape(FF, D)
    expand_full = jnp.concatenate(
        [packed[:, 120 + 24 * block : 144 + 24 * block].reshape(D, D) for block in range(4)], axis=1
    )

    branch = dot(context_tok, context_full) + context_add
    first_out, normed_one, inv_one = normalize(own.astype(F32) + branch, gain_one, shift_one)
    first_low = first_out.astype(BF16)
    expand = dot(first_low, expand_full) + expand_add
    active = smooth_gate(expand).astype(BF16)
    reduced = dot(active, reduce_full) + reduce_add
    second_out, normed_two, inv_two = normalize(first_out + reduced, gain_two, shift_two)
    hidden_out = second_out.astype(BF16)[None]

    out_rows = out_grad[0].astype(F32)
    second_gain_grad = jnp.sum(out_rows * normed_two, axis=0)
    second_shift_grad = jnp.sum(out_rows, axis=0)
    grad_two = normalize_back(out_rows, normed_two, inv_two, gain_two)
    reduced_grad = grad_two.astype(BF16)
    reduce_bias_grad = column_sum(reduced_grad)

    def spread(values):
        summed = core_sum(values, core).astype(BF16)
        return ring_sum(summed, x_at, to_x).astype(BF16)

    reduce_weight_grad = rows_first(active, reduced_grad).astype(BF16)
    reduce_part = spread(
        jnp.transpose(reduce_weight_grad.reshape(16, 2, SP, 24, D), (1, 2, 0, 3, 4))
    )

    active_grad = by_transpose(reduced_grad, reduce_full).astype(BF16)
    gate_value, gate_pullback = jax.vjp(smooth_gate, expand)
    expand_grad = gate_pullback(active_grad.astype(F32))[0].astype(BF16)
    expand_bias_grad = column_sum(expand_grad)
    expand_weight_grad = rows_first(first_low, expand_grad).astype(BF16)
    expand_part = spread(
        jnp.transpose(expand_weight_grad.reshape(16, 2, 24, SP, D), (1, 3, 0, 2, 4))
    )
    first_grad = by_transpose(expand_grad, expand_full) + grad_two
    first_gain_grad = jnp.sum(first_grad * normed_one, axis=0)
    first_shift_grad = jnp.sum(first_grad, axis=0)
    grad_one = normalize_back(first_grad, normed_one, inv_one, gain_one)
    branch_grad = grad_one.astype(BF16)
    context_bias_grad = column_sum(branch_grad)
    context_grad = by_transpose(branch_grad, context_full).astype(BF16)
    blocks = [context_grad[:, :HW]] + [None] * 3
    for step in ORDER:
        blocks[SP - step] = to_x(context_grad[:, step * HW : (step + 1) * HW], step)
    grad_heads = jnp.concatenate(blocks, axis=0)

    qkv_grad = attend_back(info, qkv, grad_heads)

    context_weight_grad = rows_first(context_tok, branch_grad).astype(BF16)
    context_weight_grad = rolled(context_weight_grad.reshape(SP, HW, D), SP - x_at)
    late_vectors = jnp.stack(
        [context_bias_grad, first_gain_grad, first_shift_grad, reduce_bias_grad, second_gain_grad, second_shift_grad],
        axis=1,
    )
    late_vectors = jnp.concatenate([late_vectors, expand_bias_grad.reshape(D, 4)], axis=1)
    side = jnp.concatenate([context_weight_grad.reshape(D, D), late_vectors.astype(BF16)], axis=1)
    side = core_sum(jnp.swapaxes(side.reshape(16, 2, 24, -1), 0, 1), core).astype(BF16)
    first_round = jnp.concatenate([reduce_part, expand_part, side], axis=-1)
    first_round = plane_sum(first_round.reshape(4, 4, 24, -1), z_at, y_at).astype(BF16)
    first_round = from_x(first_round, x_at)
    reduce_out = first_round[:, :, :D].reshape(96, D).astype(F32)
    expand_out = jnp.swapaxes(first_round[:, :, D : 2 * D], 0, 1).reshape(24, FF).astype(F32)
    side_out = jnp.sum(first_round[:, :, 2 * D :].astype(F32), axis=0)
    context_out = side_out[:, :D]
    six = side_out[:, D : D + 6].T
    expand_bias_out = side_out[:, D + 6 :].reshape(96)

    partial = by_transpose(qkv_grad, qkv_full).astype(BF16)
    input_sum = grad_one + partial[:LOCAL].astype(F32)
    for step in ORDER:
        input_sum = input_sum + to_x(partial[step * LOCAL : (step + 1) * LOCAL], step).astype(F32)
    input_grad = input_sum.astype(BF16)[None]

    qkv_weight_grad = rows_first(everyone, qkv_grad)
    sums = column_sum(qkv_grad)
    two = jnp.zeros((2, D), F32)
    two = lax.dynamic_update_slice(two, jnp.stack([sums[:HW], sums[2 * HW :]]), (0, x_at * HW))
    second_round = jnp.concatenate([qkv_weight_grad, two.T], axis=1).astype(BF16)
    second_round = core_sum(jnp.swapaxes(second_round.reshape(16, 2, 24, -1), 0, 1), core)
    second_round = plane_sum(second_round.astype(BF16).reshape(4, 4, 24, -1), z_at, y_at)
    second_round = from_x(second_round.astype(BF16), x_at).astype(F32)
    qkv_out = jnp.transpose(second_round[:, :, : 3 * HW].reshape(SP, 24, 3, HW), (1, 2, 0, 3))
    qkv_out = qkv_out.reshape(24, 3 * D)
    two_out = jnp.sum(second_round[:, :, 3 * HW :], axis=0).T

    return (
        hidden_out,
        input_grad,
        qkv_out,
        two_out[0],
        two_out[1],
        context_out,
        six[0],
        six[1],
        six[2],
        expand_out,
        expand_bias_out,
        reduce_out,
        six[3],
        six[4],
        six[5],
    )


def solution(mesh):
    sequences = P("fsdp", "sp", None)
    matrix = P("fsdp", None)
    vector = P("fsdp")
    return jax.shard_map(
        per_device,
        mesh=mesh,
        in_specs=(
            sequences, vector, matrix, vector, vector, matrix, vector, vector, vector,
            matrix, vector, matrix, vector, vector, vector, sequences,
        ),
        out_specs=(
            sequences, sequences, matrix, vector, vector, matrix, vector, vector, vector,
            matrix, vector, matrix, vector, vector, vector,
        ),
        check_vma=False,
    )
```

```python
import functools

import jax
import jax.numpy as jnp
from jax import lax
from jax.experimental import pallas as pl
from jax.experimental.pallas import tpu as pltpu
from jax.sharding import PartitionSpec as P

D = 768
H = 12
DH = 64
FF = 3072
SP = 4
LOCAL = 256
LEN = 1024
HEADS = H // SP
HW = HEADS * DH
BLOCK = 256

EPSILON = 1e-06
SCALING = 0.125
MASKED = -1000000000.0
F32 = jnp.float32
BF16 = jnp.bfloat16


def normalize(values, gain_row, shift_row):
    average = jnp.mean(values, axis=-1, keepdims=True)
    centred = values - average
    inv_std = lax.rsqrt(jnp.mean(centred * centred, axis=-1, keepdims=True) + EPSILON)
    normed = centred * inv_std
    return (normed * gain_row + shift_row, normed, inv_std)


def normalize_back(upstream, normed, inv_std, gain_row):
    weighted = upstream * gain_row
    return inv_std * (
        weighted
        - jnp.mean(weighted, axis=-1, keepdims=True)
        - normed * jnp.mean(weighted * normed, axis=-1, keepdims=True)
    )


def dot(left_side, right_side):
    return jnp.dot(left_side, right_side, preferred_element_type=F32)


def rows_first(left_side, right_side):
    return lax.dot_general(
        left_side, right_side, (((0,), (0,)), ((), ())), preferred_element_type=F32
    )


def by_transpose(left_side, right_side):
    return lax.dot_general(
        left_side, right_side, (((1,), (1,)), ((), ())), preferred_element_type=F32
    )


def smooth_gate(values):
    return jax.nn.gelu(values, approximate=True)


def column_sum(values):
    return jnp.sum(values.astype(F32), axis=0)


def to_x(values, step):
    return lax.ppermute(values, "sp", [(i, (i + step) % SP) for i in range(SP)])


ORDER = (1, 3, 2)


def rolled(values, start):
    count = values.shape[0]
    return lax.dynamic_slice_in_dim(
        jnp.concatenate([values, values], axis=0), start % count, count, axis=0
    )


def masked_keys(info_ref, shape, dim):
    at = lax.broadcasted_iota(jnp.int32, shape, dim)
    block = (info_ref[0] + lax.shift_right_logical(at, 8)) & 3
    return (block * LOCAL + (at & (LOCAL - 1))) < info_ref[1]


def attend_kernel(info_ref, qkv_ref, context_ref):
    valid = masked_keys(info_ref, (1, LEN), 1)

    @pl.loop(0, LEN // BLOCK)
    def _(step):
        rows = pl.ds(pl.multiple_of(step * BLOCK, BLOCK), BLOCK)
        outs = []
        for head in range(HEADS):
            cols = head * DH
            keys = qkv_ref[:, HW + cols : HW + cols + DH]
            vals = qkv_ref[:, 2 * HW + cols : 2 * HW + cols + DH]
            queries = qkv_ref[rows, cols : cols + DH] * jnp.asarray(SCALING, BF16)
            scores = jnp.where(valid, by_transpose(queries, keys), MASKED)
            weights = jnp.exp(scores - jnp.max(scores, axis=-1, keepdims=True))
            totals = jnp.sum(weights, axis=-1, keepdims=True)
            outs.append(dot(weights.astype(BF16), vals) * (1.0 / totals))
        context_ref[rows, :] = jnp.concatenate(outs, axis=1).astype(BF16)


def attend_back_kernel(info_ref, qkv_ref, grad_ref, out_ref, key_sum, value_sum):
    valid = masked_keys(info_ref, (LEN, 1), 0)
    key_sum[...] = jnp.zeros_like(key_sum)
    value_sum[...] = jnp.zeros_like(value_sum)

    @pl.loop(0, LEN // BLOCK)
    def _(step):
        rows = pl.ds(pl.multiple_of(step * BLOCK, BLOCK), BLOCK)
        outs = []
        for head in range(HEADS):
            cols = head * DH
            keys = qkv_ref[:, HW + cols : HW + cols + DH]
            vals = qkv_ref[:, 2 * HW + cols : 2 * HW + cols + DH]
            queries = qkv_ref[rows, cols : cols + DH] * jnp.asarray(SCALING, BF16)
            grads = grad_ref[rows, cols : cols + DH]
            scores = jnp.where(valid, by_transpose(keys, queries), MASKED)
            weights = jnp.exp(scores - jnp.max(scores, axis=0, keepdims=True))
            probs = weights * (1.0 / jnp.sum(weights, axis=0, keepdims=True))
            value_sum[head] += dot(probs.astype(BF16), grads)
            prob_grad = by_transpose(vals, grads)
            centre = jnp.sum(probs * prob_grad, axis=0, keepdims=True)
            score_grad = (probs * (prob_grad - centre)).astype(BF16)
            key_sum[head] += dot(score_grad, queries)
            outs.append(rows_first(score_grad, keys) * SCALING)
        out_ref[rows, :HW] = jnp.concatenate(outs, axis=1).astype(BF16)

    for part, total in ((1, key_sum), (2, value_sum)):
        out_ref[:, part * HW : (part + 1) * HW] = jnp.concatenate(
            [total[head] for head in range(HEADS)], axis=1
        ).astype(BF16)


def reduce_grad_kernel(active_ref, grad_ref, out_ref):
    full = rows_first(active_ref[...], grad_ref[...]).reshape(8, 4, 24, D)
    for part in range(4):
        out_ref[:, part * D : (part + 1) * D] = full[:, part].reshape(192, D).astype(BF16)


def other_grad_kernel(info_ref, first_ref, expand_ref, context_ref, branch_ref, held_ref, out_ref):
    step = pl.program_id(0)

    @pl.when(step < 4)
    def _():
        out_ref[...] = rows_first(first_ref[...], expand_ref[...]).astype(BF16)

    @pl.when(step == 4)
    def _():
        for block in range(SP):
            rows = pl.multiple_of(((info_ref[0] + block) & 3) * HW, HW)
            out_ref[pl.ds(rows, HW), :] = rows_first(
                context_ref[:, block * HW : (block + 1) * HW], branch_ref[...]
            ).astype(BF16)


SMEM = pl.BlockSpec(memory_space=pltpu.SMEM)
VMEM = pl.BlockSpec(memory_space=pltpu.VMEM)
PARAMS = pltpu.CompilerParams(vmem_limit_bytes=40 * 1024 * 1024)


def attend(info, qkv):
    return pl.pallas_call(
        attend_kernel,
        out_shape=jax.ShapeDtypeStruct((LEN, HW), BF16),
        in_specs=[SMEM, VMEM],
        out_specs=VMEM,
        compiler_params=PARAMS,
        cost_estimate=pl.CostEstimate(
            flops=4 * HEADS * LEN * LEN * 256, bytes_accessed=LEN * HW * 8, transcendentals=0
        ),
        name="attend",
    )(info, qkv)


def attend_back(info, qkv, grads):
    return pl.pallas_call(
        attend_back_kernel,
        out_shape=jax.ShapeDtypeStruct((LEN, 3 * HW), BF16),
        in_specs=[SMEM, VMEM, VMEM],
        out_specs=VMEM,
        scratch_shapes=[pltpu.VMEM((HEADS, LEN, DH), F32), pltpu.VMEM((HEADS, LEN, DH), F32)],
        compiler_params=PARAMS,
        cost_estimate=pl.CostEstimate(
            flops=10 * HEADS * LEN * LEN * 256, bytes_accessed=LEN * HW * 14, transcendentals=0
        ),
        name="attend_back",
    )(info, qkv, grads)


PACKED = 2 * FF + D


def reduce_grad(active, reduced_grad):
    return pl.pallas_call(
        reduce_grad_kernel,
        out_shape=jax.ShapeDtypeStruct((D, PACKED), BF16),
        grid=(4,),
        in_specs=[
            pl.BlockSpec((LOCAL, D), lambda i: (0, i)),
            pl.BlockSpec((LOCAL, D), lambda i: (0, 0)),
        ],
        out_specs=pl.BlockSpec((192, FF), lambda i: (i, 0)),
        compiler_params=PARAMS,
        cost_estimate=pl.CostEstimate(
            flops=2 * LOCAL * D * FF, bytes_accessed=8 * 1024 * 1024, transcendentals=0
        ),
        name="reduce_grad",
    )(active, reduced_grad)


def other_grads(info, first_low, expand_grad, context_tok, branch_grad, held):
    whole = pl.BlockSpec((LOCAL, D), lambda i: (0, 0))
    return pl.pallas_call(
        other_grad_kernel,
        out_shape=jax.ShapeDtypeStruct((D, PACKED), BF16),
        grid=(5,),
        in_specs=[
            SMEM,
            whole,
            pl.BlockSpec((LOCAL, D), lambda i: (0, jnp.minimum(i, 3))),
            whole,
            whole,
            pl.BlockSpec(memory_space=pl.ANY),
        ],
        out_specs=pl.BlockSpec((D, D), lambda i: (0, 4 + i)),
        input_output_aliases={5: 0},
        compiler_params=PARAMS,
        cost_estimate=pl.CostEstimate(
            flops=2 * LOCAL * D * (FF + D), bytes_accessed=8 * 1024 * 1024, transcendentals=0
        ),
        name="other_grads",
    )(info, first_low, expand_grad, context_tok, branch_grad, held)


def from_x(values, x_at):
    pieces = [values] + [to_x(values, -step) for step in (1, 2, 3)]
    return rolled(jnp.stack(pieces), SP - x_at)


def per_device(
    hidden_in,
    lengths,
    qkv_weight,
    query_bias,
    value_bias,
    context_weight,
    context_bias,
    first_gain,
    first_shift,
    expand_weight,
    expand_bias,
    reduce_weight,
    reduce_bias,
    second_gain,
    second_shift,
    out_grad,
):
    x_at = lax.axis_index("sp")
    own = hidden_in[0]
    tokens = [own] + [None] * 3
    for step in ORDER:
        tokens[step] = to_x(own, -step)

    row_at = lax.broadcasted_iota(jnp.int32, (8, D), 0)
    vectors = jnp.pad(expand_bias, (0, D - 96))[None]
    for row, part in enumerate(
        (context_bias, first_gain, first_shift, reduce_bias, second_gain, second_shift)
    ):
        vectors = jnp.where(row_at == row, jnp.pad(part, (0, D - 24))[None], vectors)
    packed = jnp.concatenate(
        [context_weight, reduce_weight]
        + [expand_weight[:, D * block : D * (block + 1)] for block in range(4)]
        + [vectors],
        axis=0,
    )
    packed = lax.all_gather(packed, "fsdp", axis=0, tiled=False)

    early = jnp.concatenate(
        [lax.dynamic_slice(qkv_weight, (0, part * D + x_at * HW), (24, HW)) for part in range(3)],
        axis=1,
    )
    row_at = lax.broadcasted_iota(jnp.int32, (26, 3 * HW), 0)
    early = jnp.where(
        row_at < 24,
        jnp.pad(early, ((0, 2), (0, 0))),
        jnp.where(
            row_at == 24,
            jnp.pad(query_bias, (0, 3 * HW - 24))[None],
            jnp.pad(value_bias, (0, 3 * HW - 24))[None],
        ),
    )
    early = lax.all_to_all(
        jnp.broadcast_to(early[None], (32, 26, 3 * HW)),
        "fsdp",
        split_axis=0,
        concat_axis=0,
        tiled=True,
    )
    qkv_full = early[:, :24].reshape(D, 3 * HW)
    query_full = early[:, 24, :24].reshape(D).astype(F32)
    value_full = early[:, 25, :24].reshape(D).astype(F32)

    everyone = jnp.concatenate(tokens, axis=0)
    offsets = jnp.concatenate(
        [
            lax.dynamic_slice_in_dim(query_full, x_at * HW, HW),
            jnp.zeros((HW,), F32),
            lax.dynamic_slice_in_dim(value_full, x_at * HW, HW),
        ]
    )
    qkv = (dot(everyone, qkv_full) + offsets).astype(BF16)
    info = jnp.stack([x_at.astype(jnp.int32), lengths[0]])
    context = attend(info, qkv)

    groups = [context[:LOCAL]] + [None] * 3
    for step in ORDER:
        groups[SP - step] = to_x(context[step * LOCAL : (step + 1) * LOCAL], step)
    context_tok = jnp.concatenate(groups, axis=1)

    context_full = rolled(packed[:, :24].reshape(SP, HW, D), x_at).reshape(D, D)
    reduce_full = packed[:, 24:120].reshape(FF, D)
    context_add, gain_one, shift_one, reduce_add, gain_two, shift_two = (
        packed[:, 216 + row, :24].reshape(D).astype(F32) for row in range(6)
    )
    expand_add = packed[:, 222, :96].reshape(FF).astype(F32)
    expand_full = jnp.concatenate(
        [packed[:, 120 + 24 * block : 144 + 24 * block].reshape(D, D) for block in range(4)], axis=1
    )

    branch = dot(context_tok, context_full) + context_add
    first_out, normed_one, inv_one = normalize(own.astype(F32) + branch, gain_one, shift_one)
    first_low = first_out.astype(BF16)
    expand = dot(first_low, expand_full) + expand_add
    active = smooth_gate(expand).astype(BF16)
    reduced = dot(active, reduce_full) + reduce_add
    second_out, normed_two, inv_two = normalize(first_out + reduced, gain_two, shift_two)
    hidden_out = second_out.astype(BF16)[None]

    out_rows = out_grad[0].astype(F32)
    second_gain_grad = jnp.sum(out_rows * normed_two, axis=0)
    second_shift_grad = jnp.sum(out_rows, axis=0)
    grad_two = normalize_back(out_rows, normed_two, inv_two, gain_two)
    reduced_grad = grad_two.astype(BF16)
    reduce_bias_grad = column_sum(reduced_grad)

    held = reduce_grad(active, reduced_grad)

    active_grad = by_transpose(reduced_grad, reduce_full).astype(BF16)
    gate_value, gate_pullback = jax.vjp(smooth_gate, expand)
    expand_grad = gate_pullback(active_grad.astype(F32))[0].astype(BF16)
    expand_bias_grad = column_sum(expand_grad)
    first_grad = by_transpose(expand_grad, expand_full) + grad_two
    first_gain_grad = jnp.sum(first_grad * normed_one, axis=0)
    first_shift_grad = jnp.sum(first_grad, axis=0)
    grad_one = normalize_back(first_grad, normed_one, inv_one, gain_one)
    branch_grad = grad_one.astype(BF16)
    context_bias_grad = column_sum(branch_grad)
    packed_grads = other_grads(info, first_low, expand_grad, context_tok, branch_grad, held)
    packed_grads = lax.psum_scatter(packed_grads, "fsdp", scatter_dimension=0, tiled=True)
    context_grad = by_transpose(branch_grad, context_full).astype(BF16)
    blocks = [context_grad[:, :HW]] + [None] * 3
    for step in ORDER:
        blocks[SP - step] = to_x(context_grad[:, step * HW : (step + 1) * HW], step)
    grad_heads = jnp.concatenate(blocks, axis=0)

    qkv_grad = attend_back(info, qkv, grad_heads)

    partial = by_transpose(qkv_grad, qkv_full).astype(BF16)
    input_sum = grad_one + partial[:LOCAL].astype(F32)
    for step in ORDER:
        input_sum = input_sum + to_x(partial[step * LOCAL : (step + 1) * LOCAL], step).astype(F32)
    input_grad = input_sum.astype(BF16)[None]

    qkv_weight_grad = rows_first(everyone, qkv_grad)
    sums = column_sum(qkv_grad)
    two = jnp.zeros((2, D), F32)
    two = lax.dynamic_update_slice(two, jnp.stack([sums[:HW], sums[2 * HW :]]), (0, x_at * HW))
    late = jnp.stack(
        [context_bias_grad, first_gain_grad, first_shift_grad, reduce_bias_grad, second_gain_grad, second_shift_grad],
        axis=0,
    )
    late = jnp.concatenate([two, late], axis=0).T
    second_round = jnp.concatenate([qkv_weight_grad, late, expand_bias_grad.reshape(D, 4)], axis=1)
    second_round = lax.all_to_all(
        second_round.astype(BF16).reshape(32, 24, 3 * HW + 12),
        "fsdp",
        split_axis=0,
        concat_axis=0,
        tiled=True,
    )
    second_round = jnp.sum(second_round.astype(F32), axis=0).astype(BF16)
    second_round = from_x(second_round, x_at).astype(F32)
    qkv_out = jnp.transpose(second_round[:, :, : 3 * HW].reshape(SP, 24, 3, HW), (1, 2, 0, 3))
    qkv_out = qkv_out.reshape(24, 3 * D)
    vector_out = jnp.sum(second_round[:, :, 3 * HW :], axis=0)
    eight = vector_out[:, :8].T
    expand_bias_out = vector_out[:, 8:].reshape(96)

    total = packed_grads.astype(F32)
    for step in ORDER:
        total = total + to_x(packed_grads, step).astype(F32)
    reduce_out = jnp.swapaxes(total[:, :FF].reshape(24, 4, D), 0, 1).reshape(96, D)
    expand_out = total[:, FF : 2 * FF]
    context_out = total[:, 2 * FF :]

    return (
        hidden_out,
        input_grad,
        qkv_out,
        eight[0],
        eight[1],
        context_out,
        eight[2],
        eight[3],
        eight[4],
        expand_out,
        expand_bias_out,
        reduce_out,
        eight[5],
        eight[6],
        eight[7],
    )


def solution(mesh):
    sequences = P("fsdp", "sp", None)
    matrix = P("fsdp", None)
    vector = P("fsdp")
    return jax.shard_map(
        per_device,
        mesh=mesh,
        in_specs=(
            sequences, vector, matrix, vector, vector, matrix, vector, vector, vector,
            matrix, vector, matrix, vector, vector, vector, sequences,
        ),
        out_specs=(
            sequences, sequences, matrix, vector, vector, matrix, vector, vector, vector,
            matrix, vector, matrix, vector, vector, vector,
        ),
        check_vma=False,
    )
```

```python
import jax
import jax.numpy as jnp
import numpy as np
from jax import lax
from jax.experimental import pallas as pl
from jax.experimental.pallas import tpu as pltpu
from jax.sharding import PartitionSpec as P

D = 768
H = 12
DH = 64
FF = 3072
SP = 4
LOCAL = 256
LEN = 1024
HEADS = H // SP
HW = HEADS * DH
BLOCK = 256

EPSILON = 1e-06
SCALING = 0.125
MASKED = -1000000000.0
F32 = jnp.float32
BF16 = jnp.bfloat16


def normalize(values, gain_row, shift_row):
    average = jnp.mean(values, axis=-1, keepdims=True)
    centred = values - average
    inv_std = lax.rsqrt(jnp.mean(centred * centred, axis=-1, keepdims=True) + EPSILON)
    normed = centred * inv_std
    return (normed * gain_row + shift_row, normed, inv_std)


def normalize_back(upstream, normed, inv_std, gain_row):
    weighted = upstream * gain_row
    return inv_std * (
        weighted
        - jnp.mean(weighted, axis=-1, keepdims=True)
        - normed * jnp.mean(weighted * normed, axis=-1, keepdims=True)
    )


def dot(left_side, right_side):
    return jnp.dot(left_side, right_side, preferred_element_type=F32)


def rows_first(left_side, right_side):
    return lax.dot_general(
        left_side, right_side, (((0,), (0,)), ((), ())), preferred_element_type=F32
    )


def by_transpose(left_side, right_side):
    return lax.dot_general(
        left_side, right_side, (((1,), (1,)), ((), ())), preferred_element_type=F32
    )


ROOT = 0.7978845608028654
CUBE = 0.044715


def gate_and_slope(values):
    square = values * values
    bent = jnp.tanh(ROOT * values * (1.0 + CUBE * square))
    half = 0.5 * (1.0 + bent)
    slope = half + 0.5 * values * (1.0 - bent * bent) * (ROOT * (1.0 + 3.0 * CUBE * square))
    return values * half, slope


def column_sum(values):
    return jnp.sum(values.astype(F32), axis=0)


def to_x(values, step):
    return lax.ppermute(values, "sp", [(i, (i + step) % SP) for i in range(SP)])


def to_z(values, step):
    return lax.ppermute(values, "fsdp", [(i, (i + 8 * step) % 32) for i in range(32)])


ORDER = (1, 3, 2)


def rolled(values, start):
    count = values.shape[0]
    return lax.dynamic_slice_in_dim(
        jnp.concatenate([values, values], axis=0), start % count, count, axis=0
    )


def masked_keys(info_ref, shape, dim):
    at = lax.broadcasted_iota(jnp.int32, shape, dim)
    block = (info_ref[0] + lax.shift_right_logical(at, 8)) & 3
    return (block * LOCAL + (at & (LOCAL - 1))) < info_ref[1]


def attend_kernel(info_ref, qkv_ref, context_ref):
    valid = masked_keys(info_ref, (1, LEN), 1)

    @pl.loop(0, LEN // BLOCK)
    def _(step):
        rows = pl.ds(pl.multiple_of(step * BLOCK, BLOCK), BLOCK)
        outs = []
        for head in range(HEADS):
            cols = head * DH
            keys = qkv_ref[:, HW + cols : HW + cols + DH]
            vals = qkv_ref[:, 2 * HW + cols : 2 * HW + cols + DH]
            queries = qkv_ref[rows, cols : cols + DH] * jnp.asarray(SCALING, BF16)
            scores = jnp.where(valid, by_transpose(queries, keys), MASKED)
            weights = jnp.exp(scores - jnp.max(scores, axis=-1, keepdims=True))
            totals = jnp.sum(weights, axis=-1, keepdims=True)
            outs.append(dot(weights.astype(BF16), vals) * (1.0 / totals))
        context_ref[rows, :] = jnp.concatenate(outs, axis=1).astype(BF16)


def attend_back_kernel(info_ref, qkv_ref, grad_ref, out_ref, key_sum, value_sum):
    valid = masked_keys(info_ref, (LEN, 1), 0)
    key_sum[...] = jnp.zeros_like(key_sum)
    value_sum[...] = jnp.zeros_like(value_sum)

    @pl.loop(0, LEN // BLOCK)
    def _(step):
        rows = pl.ds(pl.multiple_of(step * BLOCK, BLOCK), BLOCK)
        outs = []
        for head in range(HEADS):
            cols = head * DH
            keys = qkv_ref[:, HW + cols : HW + cols + DH]
            vals = qkv_ref[:, 2 * HW + cols : 2 * HW + cols + DH]
            queries = qkv_ref[rows, cols : cols + DH] * jnp.asarray(SCALING, BF16)
            grads = grad_ref[rows, cols : cols + DH]
            scores = jnp.where(valid, by_transpose(keys, queries), MASKED)
            weights = jnp.exp(scores - jnp.max(scores, axis=0, keepdims=True))
            probs = weights * (1.0 / jnp.sum(weights, axis=0, keepdims=True))
            value_sum[head] += dot(probs.astype(BF16), grads)
            prob_grad = by_transpose(vals, grads)
            centre = jnp.sum(probs * prob_grad, axis=0, keepdims=True)
            score_grad = (probs * (prob_grad - centre)).astype(BF16)
            key_sum[head] += dot(score_grad, queries)
            outs.append(rows_first(score_grad, keys) * SCALING)
        out_ref[rows, :HW] = jnp.concatenate(outs, axis=1).astype(BF16)

    for part, total in ((1, key_sum), (2, value_sum)):
        out_ref[:, part * HW : (part + 1) * HW] = jnp.concatenate(
            [total[head] for head in range(HEADS)], axis=1
        ).astype(BF16)


PACKED = 2 * FF + D


def reorder_matrix():
    source = np.arange(D).reshape(8, 4, 24).transpose(1, 0, 2).reshape(D)
    matrix = np.zeros((D, D), np.float32)
    matrix[source, np.arange(D)] = 1.0
    return matrix


def pack_kernel(info_ref, *rest):
    sources, (packed_ref, early_ref), held = rest[:14], rest[14:16], rest[16:30]
    rows_ref, sems = rest[30:]
    fetches = [
        pltpu.make_async_copy(source, target, sems.at[at])
        for at, (source, target) in enumerate(zip(sources, held))
    ]
    for fetch in fetches:
        fetch.start()
    qkv_ref, context_ref, expand_ref, reduce_ref, order_ref = held[:5]
    vector_refs = held[5:]
    for fetch in fetches:
        fetch.wait()
    reduce_rows = reduce_ref[...].astype(F32)
    for part in range(4):
        packed_ref[:, part * D : (part + 1) * D] = reduce_rows[part * 24 : (part + 1) * 24].astype(BF16)
    moved = [dot(expand_ref[:, q * D : (q + 1) * D], order_ref[...]) for q in range(4)]
    for part in range(4):
        packed_ref[:, FF + part * D : FF + (part + 1) * D] = jnp.concatenate(
            [values[:, part * HW : (part + 1) * HW] for values in moved], axis=1
        ).astype(BF16)
    packed_ref[:, 2 * FF :] = context_ref[...]

    rows_ref[...] = jnp.zeros_like(rows_ref)
    for row in range(8):
        rows_ref[row : row + 1, :24] = vector_refs[row][...].astype(F32).reshape(1, 24)
    rows_ref[0:1, 128:224] = vector_refs[8][...].astype(F32).reshape(1, 96)
    for at in range(SP):

        @pl.when(info_ref[0] == at)
        def _(at=at):
            own = jnp.concatenate(
                [qkv_ref[:, part * D + at * HW : part * D + (at + 1) * HW] for part in range(3)],
                axis=1,
            )
            block = jnp.concatenate([own.astype(F32), rows_ref[...]], axis=0).astype(BF16)

            @pl.loop(0, 32)
            def _(owner):
                early_ref[owner] = block


def middle_kernel(
    info_ref, context_ref, own_ref, cotangent_ref, rows_ref, bias_ref, weights_ref,
    hidden_ref, grad_one_ref, context_grad_ref, sums_ref, bias_sum_ref, grads_ref,
    held, made, slopes, active, in_sems, out_sems,
):
    def piece(block):
        return slice(block * D, (block + 1) * D)

    copies = {}
    for block in (8, 4, 0, 5, 1, 6, 2, 7, 3):
        copies[block] = pltpu.make_async_copy(
            weights_ref.at[:, piece(block)], held.at[:, piece(block)], in_sems.at[block]
        )
        copies[block].start()

    def send(block):
        copy = pltpu.make_async_copy(
            made.at[:, piece(block)], grads_ref.at[:, piece(block)], out_sems.at[block]
        )
        copy.start()
        return copy

    context_add, gain_one, shift_one, reduce_add, gain_two, shift_two = (
        rows_ref[row : row + 1, :] for row in range(2, 8)
    )
    groups = [(z - info_ref[0]) & 3 for z in range(SP)]

    def by_plane(values):
        return jnp.concatenate(
            [values[(8 * z + m) * 24 : (8 * z + m + 1) * 24] for m in range(8) for z in range(4)],
            axis=0,
        ).astype(BF16)

    own = own_ref[...].astype(F32) + context_add
    copies[8].wait()
    for block in range(SP):
        own = own + dot(
            context_ref[groups[block]], held[block * HW : (block + 1) * HW, piece(8)]
        )
    first_out, normed_one, inv_one = normalize(own, gain_one, shift_one)
    first_low = first_out.astype(BF16)
    second_in = first_out + reduce_add
    for part in range(4):
        copies[4 + part].wait()
        expand = dot(first_low, held[:, piece(4 + part)]) + bias_ref[:, piece(part)]
        value, slope = gate_and_slope(expand)
        active[:, piece(part)] = value.astype(BF16)
        slopes[:, piece(part)] = slope
        copies[part].wait()
        second_in = second_in + dot(active[:, piece(part)], held[:, piece(part)])
    second_out, normed_two, inv_two = normalize(second_in, gain_two, shift_two)
    hidden_ref[...] = second_out.astype(BF16)

    cotangent = cotangent_ref[...].astype(F32)
    grad_two = normalize_back(cotangent, normed_two, inv_two, gain_two)
    reduced_grad = grad_two.astype(BF16)
    sums_ref[...] = jnp.zeros_like(sums_ref)
    sums_ref[3:4, :] = jnp.sum(reduced_grad.astype(F32), axis=0, keepdims=True)
    sums_ref[4:5, :] = jnp.sum(cotangent * normed_two, axis=0, keepdims=True)
    sums_ref[5:6, :] = jnp.sum(cotangent, axis=0, keepdims=True)
    first_grad = grad_two
    sent = []
    for part in range(4):
        active_grad = by_transpose(reduced_grad, held[:, piece(part)]).astype(BF16)
        expand_grad = (active_grad.astype(F32) * slopes[:, piece(part)]).astype(BF16)
        bias_sum_ref[part : part + 1, :] = jnp.sum(expand_grad.astype(F32), axis=0, keepdims=True)
        first_grad = first_grad + by_transpose(expand_grad, held[:, piece(4 + part)])
        made[:, piece(part)] = by_plane(rows_first(active[:, piece(part)], reduced_grad))
        sent.append(send(part))
        made[:, piece(4 + part)] = by_plane(rows_first(first_low, expand_grad))
        sent.append(send(4 + part))
    sums_ref[1:2, :] = jnp.sum(first_grad * normed_one, axis=0, keepdims=True)
    sums_ref[2:3, :] = jnp.sum(first_grad, axis=0, keepdims=True)
    grad_one = normalize_back(first_grad, normed_one, inv_one, gain_one)
    grad_one_ref[...] = grad_one
    branch_grad = grad_one.astype(BF16)
    sums_ref[0:1, :] = jnp.sum(branch_grad.astype(F32), axis=0, keepdims=True)
    made[:, piece(8)] = by_plane(
        jnp.concatenate([rows_first(context_ref[group], branch_grad) for group in groups], axis=0)
    )
    sent.append(send(8))
    for block in range(SP):
        context_grad_ref[groups[block]] = by_transpose(
            branch_grad, held[block * HW : (block + 1) * HW, piece(8)]
        ).astype(BF16)
    for copy in sent:
        copy.wait()


SMEM = pl.BlockSpec(memory_space=pltpu.SMEM)
VMEM = pl.BlockSpec(memory_space=pltpu.VMEM)
PARAMS = pltpu.CompilerParams(vmem_limit_bytes=40 * 1024 * 1024)


def attend(info, qkv):
    return pl.pallas_call(
        attend_kernel,
        out_shape=jax.ShapeDtypeStruct((LEN, HW), BF16),
        in_specs=[SMEM, VMEM],
        out_specs=VMEM,
        compiler_params=PARAMS,
        cost_estimate=pl.CostEstimate(
            flops=4 * HEADS * LEN * LEN * 256, bytes_accessed=LEN * HW * 8, transcendentals=0
        ),
        name="attend",
    )(info, qkv)


def attend_back(info, qkv, grads):
    return pl.pallas_call(
        attend_back_kernel,
        out_shape=jax.ShapeDtypeStruct((LEN, 3 * HW), BF16),
        in_specs=[SMEM, VMEM, VMEM],
        out_specs=VMEM,
        scratch_shapes=[pltpu.VMEM((HEADS, LEN, DH), F32), pltpu.VMEM((HEADS, LEN, DH), F32)],
        compiler_params=PARAMS,
        cost_estimate=pl.CostEstimate(
            flops=10 * HEADS * LEN * LEN * 256, bytes_accessed=LEN * HW * 14, transcendentals=0
        ),
        name="attend_back",
    )(info, qkv, grads)


def pack(info, qkv_weight, context_weight, expand_weight, reduce_weight, vectors):
    operands = (
        qkv_weight, context_weight, expand_weight, reduce_weight,
        jnp.asarray(reorder_matrix(), BF16), *vectors,
    )
    return pl.pallas_call(
        pack_kernel,
        out_shape=(
            jax.ShapeDtypeStruct((24, PACKED), BF16),
            jax.ShapeDtypeStruct((32, 32, 3 * HW), BF16),
        ),
        in_specs=[SMEM] + [pl.BlockSpec(memory_space=pltpu.HBM)] * len(operands),
        out_specs=(VMEM, VMEM),
        scratch_shapes=[pltpu.VMEM(operand.shape, BF16) for operand in operands]
        + [pltpu.VMEM((8, 3 * HW), F32), pltpu.SemaphoreType.DMA((len(operands),))],
        compiler_params=pltpu.CompilerParams(vmem_limit_bytes=60 * 1024 * 1024),
        name="pack",
    )(info, *operands)


def finish_kernel(a_ref, b_ref, c_ref, d_ref, order_ref, reduce_ref, expand_ref, context_ref):
    def total(start, width):
        parts = [ref[:, start : start + width].astype(F32) for ref in (a_ref, b_ref, c_ref, d_ref)]
        return (parts[0] + parts[1]) + (parts[2] + parts[3])

    for part in range(4):
        reduce_ref[part * 24 : (part + 1) * 24, :] = total(part * D, D)
    context_ref[...] = total(2 * FF, D)
    moved = [total(FF + part * D, D) for part in range(4)]
    for q in range(4):
        left = jnp.concatenate([values[:, q * HW : (q + 1) * HW] for values in moved], axis=1)
        result = jnp.zeros((24, D), F32)
        for _ in range(3):
            term = left.astype(BF16)
            result = result + by_transpose(term, order_ref[...])
            left = left - term.astype(F32)
        expand_ref[:, q * D : (q + 1) * D] = result


def finish(pieces):
    return pl.pallas_call(
        finish_kernel,
        out_shape=(
            jax.ShapeDtypeStruct((96, D), F32),
            jax.ShapeDtypeStruct((24, FF), F32),
            jax.ShapeDtypeStruct((24, D), F32),
        ),
        in_specs=[VMEM] * 5,
        out_specs=(VMEM,) * 3,
        compiler_params=PARAMS,
        name="finish",
    )(*pieces, jnp.asarray(reorder_matrix(), BF16))


def middle(info, context_tok, own, cotangent, rows, bias, weights):
    tall = (LOCAL, D)
    return pl.pallas_call(
        middle_kernel,
        out_shape=(
            jax.ShapeDtypeStruct(tall, BF16),
            jax.ShapeDtypeStruct(tall, F32),
            jax.ShapeDtypeStruct((SP, LOCAL, HW), BF16),
            jax.ShapeDtypeStruct((8, D), F32),
            jax.ShapeDtypeStruct((4, D), F32),
            jax.ShapeDtypeStruct((D, PACKED), BF16),
        ),
        in_specs=[SMEM] + [VMEM] * 5 + [pl.BlockSpec(memory_space=pl.ANY)],
        out_specs=(VMEM,) * 5 + (pl.BlockSpec(memory_space=pl.ANY),),
        scratch_shapes=[
            pltpu.VMEM((D, PACKED), BF16),
            pltpu.VMEM((D, PACKED), BF16),
            pltpu.VMEM((LOCAL, FF), F32),
            pltpu.VMEM((LOCAL, FF), BF16),
            pltpu.SemaphoreType.DMA((9,)),
            pltpu.SemaphoreType.DMA((9,)),
        ],
        compiler_params=pltpu.CompilerParams(vmem_limit_bytes=48 * 1024 * 1024),
        cost_estimate=pl.CostEstimate(
            flops=6 * LOCAL * D * PACKED, bytes_accessed=24 * 1024 * 1024, transcendentals=0
        ),
        name="middle",
    )(info, context_tok, own, cotangent, rows, bias, weights)


def from_x(values, x_at):
    pieces = [values] + [to_x(values, -step) for step in (1, 2, 3)]
    return rolled(jnp.stack(pieces), SP - x_at)


def per_device(
    hidden_in,
    lengths,
    qkv_weight,
    query_bias,
    value_bias,
    context_weight,
    context_bias,
    first_gain,
    first_shift,
    expand_weight,
    expand_bias,
    reduce_weight,
    reduce_bias,
    second_gain,
    second_shift,
    out_grad,
):
    x_at = lax.axis_index("sp")
    own = hidden_in[0]
    tokens = [own] + [None] * 3
    for step in ORDER:
        tokens[step] = to_x(own, -step)

    info = jnp.stack([x_at.astype(jnp.int32), lengths[0]])
    packed, early = pack(
        info, qkv_weight, context_weight, expand_weight, reduce_weight,
        (query_bias, value_bias, context_bias, first_gain, first_shift, reduce_bias,
         second_gain, second_shift, expand_bias),
    )
    packed = lax.all_gather(packed, "fsdp", axis=0, tiled=True)
    early = lax.all_to_all(early, "fsdp", split_axis=0, concat_axis=0, tiled=True)
    qkv_full = early[:, :24].reshape(D, 3 * HW)
    rows = jnp.swapaxes(early[:, 24:, :24], 0, 1).reshape(8, D).astype(F32)
    query_full, value_full = rows[0], rows[1]
    expand_add = jnp.swapaxes(early[:, 24, 128:224].reshape(32, 4, 24), 0, 1)
    expand_add = expand_add.reshape(1, FF).astype(F32)

    everyone = jnp.concatenate(tokens, axis=0)
    offsets = jnp.concatenate(
        [
            lax.dynamic_slice_in_dim(query_full, x_at * HW, HW),
            jnp.zeros((HW,), F32),
            lax.dynamic_slice_in_dim(value_full, x_at * HW, HW),
        ]
    )
    qkv = (dot(everyone, qkv_full) + offsets).astype(BF16)
    context = attend(info, qkv)

    groups = [context[:LOCAL]] + [None] * 3
    for step in ORDER:
        groups[SP - step] = to_x(context[step * LOCAL : (step + 1) * LOCAL], step)
    context_tok = jnp.stack(groups)

    hidden_out, grad_one, context_grad, row_sums, bias_sums, packed_grads = middle(
        info, context_tok, own, out_grad[0], rows, expand_add, packed
    )
    packed_grads = lax.psum_scatter(
        packed_grads,
        "fsdp",
        scatter_dimension=0,
        axis_index_groups=[[8 * z + m for m in range(8)] for z in range(4)],
        tiled=True,
    )
    z_at = lax.axis_index("fsdp") // 8

    def rows_of(step):
        return lax.dynamic_slice_in_dim(packed_grads, (z_at + step) % 4 * 24, 24, axis=0)

    z_sum = rows_of(0).astype(F32)
    for step in ORDER:
        z_sum = z_sum + to_z(rows_of(step), step).astype(F32)
    packed_grads = z_sum.astype(BF16)
    blocks = [context_grad[0]] + [None] * 3
    for step in ORDER:
        blocks[SP - step] = to_x(context_grad[step], step)
    grad_heads = jnp.concatenate(blocks, axis=0)

    qkv_grad = attend_back(info, qkv, grad_heads)

    partial = by_transpose(qkv_grad, qkv_full).astype(BF16)
    input_sum = grad_one + partial[:LOCAL].astype(F32)
    for step in ORDER:
        input_sum = input_sum + to_x(partial[step * LOCAL : (step + 1) * LOCAL], step).astype(F32)
    input_grad = input_sum.astype(BF16)[None]

    qkv_weight_grad = rows_first(everyone, qkv_grad)
    sums = column_sum(qkv_grad)
    two = jnp.zeros((2, D), F32)
    two = lax.dynamic_update_slice(two, jnp.stack([sums[:HW], sums[2 * HW :]]), (0, x_at * HW))
    late = jnp.concatenate([two, row_sums[:6], bias_sums], axis=0).T
    second_round = jnp.concatenate([qkv_weight_grad, late], axis=1)
    second_round = lax.all_to_all(
        second_round.astype(BF16).reshape(32, 24, 3 * HW + 12),
        "fsdp",
        split_axis=0,
        concat_axis=0,
        tiled=True,
    )
    second_round = jnp.sum(second_round.astype(F32), axis=0).astype(BF16)
    second_round = from_x(second_round, x_at).astype(F32)
    qkv_out = jnp.transpose(second_round[:, :, : 3 * HW].reshape(SP, 24, 3, HW), (1, 2, 0, 3))
    qkv_out = qkv_out.reshape(24, 3 * D)
    vector_out = jnp.sum(second_round[:, :, 3 * HW :], axis=0)
    eight = vector_out.T
    expand_bias_out = eight[8:].reshape(96)

    reduce_out, expand_out, context_out = finish(
        [packed_grads] + [to_x(packed_grads, step) for step in ORDER]
    )

    return (
        hidden_out[None],
        input_grad,
        qkv_out,
        eight[0],
        eight[1],
        context_out,
        eight[2],
        eight[3],
        eight[4],
        expand_out,
        expand_bias_out,
        reduce_out,
        eight[5],
        eight[6],
        eight[7],
    )


def solution(mesh):
    sequences = P("fsdp", "sp", None)
    matrix = P("fsdp", None)
    vector = P("fsdp")
    return jax.shard_map(
        per_device,
        mesh=mesh,
        in_specs=(
            sequences, vector, matrix, vector, vector, matrix, vector, vector, vector,
            matrix, vector, matrix, vector, vector, vector, sequences,
        ),
        out_specs=(
            sequences, sequences, matrix, vector, vector, matrix, vector, vector, vector,
            matrix, vector, matrix, vector, vector, vector,
        ),
        check_vma=False,
    )
```

```python
import jax
import jax.numpy as jnp
import numpy as np
from jax import lax
from jax.experimental import pallas as pl
from jax.experimental.pallas import tpu as pltpu
from jax.sharding import PartitionSpec as P

D = 768
H = 12
DH = 64
FF = 3072
SP = 4
LOCAL = 256
LEN = 1024
HEADS = H // SP
HW = HEADS * DH
BLOCK = 256

EPSILON = 1e-06
SCALING = 0.125
MASKED = -1000000000.0
F32 = jnp.float32
BF16 = jnp.bfloat16


def normalize(values, gain_row, shift_row):
    average = jnp.mean(values, axis=-1, keepdims=True)
    centred = values - average
    inv_std = lax.rsqrt(jnp.mean(centred * centred, axis=-1, keepdims=True) + EPSILON)
    normed = centred * inv_std
    return (normed * gain_row + shift_row, normed, inv_std)


def normalize_back(upstream, normed, inv_std, gain_row):
    weighted = upstream * gain_row
    return inv_std * (
        weighted
        - jnp.mean(weighted, axis=-1, keepdims=True)
        - normed * jnp.mean(weighted * normed, axis=-1, keepdims=True)
    )


def dot(left_side, right_side):
    return jnp.dot(left_side, right_side, preferred_element_type=F32)


def rows_first(left_side, right_side):
    return lax.dot_general(
        left_side, right_side, (((0,), (0,)), ((), ())), preferred_element_type=F32
    )


def by_transpose(left_side, right_side):
    return lax.dot_general(
        left_side, right_side, (((1,), (1,)), ((), ())), preferred_element_type=F32
    )


ROOT = 0.7978845608028654
CUBE = 0.044715


def gate_and_slope(values):
    square = values * values
    bent = jnp.tanh(ROOT * values * (1.0 + CUBE * square))
    half = 0.5 * (1.0 + bent)
    slope = half + 0.5 * values * (1.0 - bent * bent) * (ROOT * (1.0 + 3.0 * CUBE * square))
    return values * half, slope


def to_x(values, step):
    return lax.ppermute(values, "sp", [(i, (i + step) % SP) for i in range(SP)])


def to_z(values, step):
    return lax.ppermute(values, "fsdp", [(i, (i + 8 * step) % 32) for i in range(32)])


ORDER = (1, 3, 2)


def rolled(values, start):
    count = values.shape[0]
    return lax.dynamic_slice_in_dim(
        jnp.concatenate([values, values], axis=0), start % count, count, axis=0
    )


def masked_keys(info_ref, shape, dim):
    at = lax.broadcasted_iota(jnp.int32, shape, dim)
    block = (info_ref[0] + lax.shift_right_logical(at, 8)) & 3
    return (block * LOCAL + (at & (LOCAL - 1))) < info_ref[1]


def attend_kernel(info_ref, qkv_ref, context_ref):
    valid = masked_keys(info_ref, (1, LEN), 1)

    @pl.loop(0, LEN // BLOCK)
    def _(step):
        rows = pl.ds(pl.multiple_of(step * BLOCK, BLOCK), BLOCK)
        outs = []
        for head in range(HEADS):
            cols = head * DH
            keys = qkv_ref[:, HW + cols : HW + cols + DH]
            vals = qkv_ref[:, 2 * HW + cols : 2 * HW + cols + DH]
            queries = qkv_ref[rows, cols : cols + DH] * jnp.asarray(SCALING, BF16)
            scores = jnp.where(valid, by_transpose(queries, keys), MASKED)
            weights = jnp.exp(scores - jnp.max(scores, axis=-1, keepdims=True))
            totals = jnp.sum(weights, axis=-1, keepdims=True)
            outs.append(dot(weights.astype(BF16), vals) * (1.0 / totals))
        context_ref[rows, :] = jnp.concatenate(outs, axis=1).astype(BF16)


def attend_back_kernel(
    info_ref, qkv_ref, grad_ref, tokens_ref, context_ref, sums_ref, bias_sum_ref,
    out_ref, late_ref, key_sum, value_sum, stack,
):
    valid = masked_keys(info_ref, (LEN, 1), 0)
    key_sum[...] = jnp.zeros_like(key_sum)
    value_sum[...] = jnp.zeros_like(value_sum)

    @pl.loop(0, LEN // BLOCK)
    def _(step):
        rows = pl.ds(pl.multiple_of(step * BLOCK, BLOCK), BLOCK)
        outs = []
        for head in range(HEADS):
            cols = head * DH
            keys = qkv_ref[:, HW + cols : HW + cols + DH]
            vals = qkv_ref[:, 2 * HW + cols : 2 * HW + cols + DH]
            queries = qkv_ref[rows, cols : cols + DH] * jnp.asarray(SCALING, BF16)
            grads = grad_ref[rows, cols : cols + DH]
            scores = jnp.where(valid, by_transpose(keys, queries), MASKED)
            weights = jnp.exp(scores - jnp.max(scores, axis=0, keepdims=True))
            probs = weights * (1.0 / jnp.sum(weights, axis=0, keepdims=True))
            value_sum[head] += dot(probs.astype(BF16), grads)
            prob_grad = by_transpose(vals, grads)
            centre = jnp.sum(probs * prob_grad, axis=0, keepdims=True)
            score_grad = (probs * (prob_grad - centre)).astype(BF16)
            key_sum[head] += dot(score_grad, queries)
            outs.append(rows_first(score_grad, keys) * SCALING)
        out_ref[rows, :HW] = jnp.concatenate(outs, axis=1).astype(BF16)

    for part, total in ((1, key_sum), (2, value_sum)):
        out_ref[:, part * HW : (part + 1) * HW] = jnp.concatenate(
            [total[head] for head in range(HEADS)], axis=1
        ).astype(BF16)

    low = out_ref[...]
    late_ref[:, D + 128 :] = rows_first(tokens_ref[...], low).astype(BF16)
    late_ref[:, :D] = context_ref[...]
    sums = jnp.sum(low.astype(F32), axis=0, keepdims=True)
    stack[...] = jnp.zeros_like(stack)
    for row, part in ((0, 0), (1, 2)):
        own = sums[:, part * HW : (part + 1) * HW]
        stack[row : row + 1, :] = jnp.concatenate(
            [jnp.where(info_ref[0] == at, own, 0.0) for at in range(SP)], axis=1
        )
    stack[2:8, :] = sums_ref[0:6, :]
    stack[8:12, :] = bias_sum_ref[...]
    late_ref[:, D : D + 128] = stack[...].T.astype(BF16)


PACKED = 2 * FF + D
LATE = D + 128 + 3 * HW


def reorder_matrix():
    source = np.arange(D).reshape(8, 4, 24).transpose(1, 0, 2).reshape(D)
    matrix = np.zeros((D, D), np.float32)
    matrix[source, np.arange(D)] = 1.0
    return matrix


def pack_kernel(info_ref, *rest):
    sources, (packed_ref, early_ref), held = rest[:14], rest[14:16], rest[16:30]
    rows_ref, sems = rest[30:]
    fetches = [
        pltpu.make_async_copy(source, target, sems.at[at])
        for at, (source, target) in enumerate(zip(sources, held))
    ]
    for fetch in fetches:
        fetch.start()
    qkv_ref, context_ref, expand_ref, reduce_ref, order_ref = held[:5]
    vector_refs = held[5:]
    for fetch in fetches:
        fetch.wait()
    reduce_rows = reduce_ref[...].astype(F32)
    for part in range(4):
        packed_ref[:, part * D : (part + 1) * D] = reduce_rows[part * 24 : (part + 1) * 24].astype(BF16)
    stacked = jnp.concatenate(
        [expand_ref[:, q * D : (q + 1) * D].astype(F32) for q in range(4)], axis=0
    )
    stacked = dot(stacked.astype(BF16), order_ref[...])
    moved = [stacked[q * 24 : (q + 1) * 24] for q in range(4)]
    for part in range(4):
        packed_ref[:, FF + part * D : FF + (part + 1) * D] = jnp.concatenate(
            [values[:, part * HW : (part + 1) * HW] for values in moved], axis=1
        ).astype(BF16)
    packed_ref[:, 2 * FF :] = context_ref[...]

    rows_ref[...] = jnp.zeros_like(rows_ref)
    for row in range(8):
        rows_ref[row : row + 1, :24] = vector_refs[row][...].astype(F32).reshape(1, 24)
    rows_ref[0:1, 128:224] = vector_refs[8][...].astype(F32).reshape(1, 96)
    for at in range(SP):

        @pl.when(info_ref[0] == at)
        def _(at=at):
            own = jnp.concatenate(
                [qkv_ref[:, part * D + at * HW : part * D + (at + 1) * HW] for part in range(3)],
                axis=1,
            )
            block = jnp.concatenate([own.astype(F32), rows_ref[...]], axis=0).astype(BF16)

            @pl.loop(0, 32)
            def _(owner):
                early_ref[owner] = block


def middle_kernel(
    info_ref, context_ref, own_ref, cotangent_ref, rows_ref, bias_ref, weights_ref,
    hidden_ref, grad_one_ref, context_grad_ref, sums_ref, bias_sum_ref, context_sum_ref, grads_ref,
    held, made, slopes, active, in_sems, out_sems,
):
    def piece(block):
        return slice(block * D, (block + 1) * D)

    copies = {}
    for block in (8, 4, 0, 5, 1, 6, 2, 7, 3):
        copies[block] = pltpu.make_async_copy(
            weights_ref.at[:, piece(block)], held.at[:, piece(block)], in_sems.at[block]
        )
        copies[block].start()

    def send(block):
        copy = pltpu.make_async_copy(
            made.at[:, piece(block)], grads_ref.at[:, piece(block)], out_sems.at[block]
        )
        copy.start()
        return copy

    context_add, gain_one, shift_one, reduce_add, gain_two, shift_two = (
        rows_ref[row : row + 1, :] for row in range(2, 8)
    )
    groups = [(z - info_ref[0]) & 3 for z in range(SP)]

    def by_plane(values):
        return jnp.concatenate(
            [values[(8 * z + m) * 24 : (8 * z + m + 1) * 24] for m in range(8) for z in range(4)],
            axis=0,
        ).astype(BF16)

    own = own_ref[...].astype(F32) + context_add
    copies[8].wait()
    for block in range(SP):
        own = own + dot(
            context_ref[groups[block]], held[block * HW : (block + 1) * HW, piece(8)]
        )
    first_out, normed_one, inv_one = normalize(own, gain_one, shift_one)
    first_low = first_out.astype(BF16)
    second_in = first_out + reduce_add
    for part in range(4):
        copies[4 + part].wait()
        expand = dot(first_low, held[:, piece(4 + part)]) + bias_ref[:, piece(part)]
        value, slope = gate_and_slope(expand)
        active[:, piece(part)] = value.astype(BF16)
        slopes[:, piece(part)] = slope
        copies[part].wait()
        second_in = second_in + dot(active[:, piece(part)], held[:, piece(part)])
    second_out, normed_two, inv_two = normalize(second_in, gain_two, shift_two)
    hidden_ref[...] = second_out.astype(BF16)

    cotangent = cotangent_ref[...].astype(F32)
    grad_two = normalize_back(cotangent, normed_two, inv_two, gain_two)
    reduced_grad = grad_two.astype(BF16)
    sums_ref[...] = jnp.zeros_like(sums_ref)
    sums_ref[3:4, :] = jnp.sum(reduced_grad.astype(F32), axis=0, keepdims=True)
    sums_ref[4:5, :] = jnp.sum(cotangent * normed_two, axis=0, keepdims=True)
    sums_ref[5:6, :] = jnp.sum(cotangent, axis=0, keepdims=True)
    first_grad = grad_two
    sent = []
    for part in range(4):
        active_grad = by_transpose(reduced_grad, held[:, piece(part)]).astype(BF16)
        expand_grad = (active_grad.astype(F32) * slopes[:, piece(part)]).astype(BF16)
        bias_sum_ref[part : part + 1, :] = jnp.sum(expand_grad.astype(F32), axis=0, keepdims=True)
        first_grad = first_grad + by_transpose(expand_grad, held[:, piece(4 + part)])
        made[:, piece(part)] = by_plane(rows_first(active[:, piece(part)], reduced_grad))
        sent.append(send(part))
        made[:, piece(4 + part)] = by_plane(rows_first(first_low, expand_grad))
        sent.append(send(4 + part))
    sums_ref[1:2, :] = jnp.sum(first_grad * normed_one, axis=0, keepdims=True)
    sums_ref[2:3, :] = jnp.sum(first_grad, axis=0, keepdims=True)
    grad_one = normalize_back(first_grad, normed_one, inv_one, gain_one)
    grad_one_ref[...] = grad_one
    branch_grad = grad_one.astype(BF16)
    sums_ref[0:1, :] = jnp.sum(branch_grad.astype(F32), axis=0, keepdims=True)
    for block in range(SP):
        context_sum_ref[block * HW : (block + 1) * HW, :] = rows_first(
            context_ref[groups[block]], branch_grad
        ).astype(BF16)
    for block in range(SP):
        context_grad_ref[groups[block]] = by_transpose(
            branch_grad, held[block * HW : (block + 1) * HW, piece(8)]
        ).astype(BF16)
    for copy in sent:
        copy.wait()


SMEM = pl.BlockSpec(memory_space=pltpu.SMEM)
VMEM = pl.BlockSpec(memory_space=pltpu.VMEM)
PARAMS = pltpu.CompilerParams(vmem_limit_bytes=40 * 1024 * 1024)


def attend(info, qkv):
    return pl.pallas_call(
        attend_kernel,
        out_shape=jax.ShapeDtypeStruct((LEN, HW), BF16),
        in_specs=[SMEM, VMEM],
        out_specs=VMEM,
        compiler_params=PARAMS,
        cost_estimate=pl.CostEstimate(
            flops=4 * HEADS * LEN * LEN * 256, bytes_accessed=LEN * HW * 8, transcendentals=0
        ),
        name="attend",
    )(info, qkv)


def attend_back(info, qkv, grads, tokens, context_sum, row_sums, bias_sums):
    return pl.pallas_call(
        attend_back_kernel,
        out_shape=(
            jax.ShapeDtypeStruct((LEN, 3 * HW), BF16),
            jax.ShapeDtypeStruct((D, LATE), BF16),
        ),
        in_specs=[SMEM] + [VMEM] * 6,
        out_specs=(VMEM, VMEM),
        scratch_shapes=[
            pltpu.VMEM((HEADS, LEN, DH), F32),
            pltpu.VMEM((HEADS, LEN, DH), F32),
            pltpu.VMEM((128, D), F32),
        ],
        compiler_params=PARAMS,
        cost_estimate=pl.CostEstimate(
            flops=10 * HEADS * LEN * LEN * 256, bytes_accessed=LEN * HW * 14, transcendentals=0
        ),
        name="attend_back",
    )(info, qkv, grads, tokens, context_sum, row_sums, bias_sums)


def pack(info, qkv_weight, context_weight, expand_weight, reduce_weight, vectors):
    operands = (
        qkv_weight, context_weight, expand_weight, reduce_weight,
        jnp.asarray(reorder_matrix(), BF16), *vectors,
    )
    return pl.pallas_call(
        pack_kernel,
        out_shape=(
            jax.ShapeDtypeStruct((24, PACKED), BF16),
            jax.ShapeDtypeStruct((32, 32, 3 * HW), BF16),
        ),
        in_specs=[SMEM] + [pl.BlockSpec(memory_space=pltpu.HBM)] * len(operands),
        out_specs=(VMEM, VMEM),
        scratch_shapes=[pltpu.VMEM(operand.shape, BF16) for operand in operands]
        + [pltpu.VMEM((8, 3 * HW), F32), pltpu.SemaphoreType.DMA((len(operands),))],
        compiler_params=pltpu.CompilerParams(vmem_limit_bytes=60 * 1024 * 1024),
        name="pack",
    )(info, *operands)


def add_up_kernel(parts_ref, after_ref, out_ref):
    total = parts_ref[0].astype(F32)
    for owner in range(1, 32):
        total = total + parts_ref[owner].astype(F32)
    out_ref[...] = total.astype(BF16)


def add_up(parts, after):
    return pl.pallas_call(
        add_up_kernel,
        out_shape=jax.ShapeDtypeStruct(parts.shape[1:], BF16),
        in_specs=[VMEM, pl.BlockSpec(memory_space=pl.ANY)],
        out_specs=VMEM,
        compiler_params=PARAMS,
        cost_estimate=pl.CostEstimate(
            flops=parts.size, bytes_accessed=2 * parts.size, transcendentals=0
        ),
        name="add_up",
    )(parts, after)


def finish_kernel(a_ref, b_ref, c_ref, d_ref, order_ref, reduce_ref, expand_ref):
    def total(start, width):
        parts = [ref[:, start : start + width].astype(F32) for ref in (a_ref, b_ref, c_ref, d_ref)]
        return (parts[0] + parts[1]) + (parts[2] + parts[3])

    for part in range(4):
        reduce_ref[part * 24 : (part + 1) * 24, :] = total(part * D, D)
    moved = [total(FF + part * D, D) for part in range(4)]
    left = jnp.concatenate(
        [
            jnp.concatenate([values[:, q * HW : (q + 1) * HW] for values in moved], axis=1)
            for q in range(4)
        ],
        axis=0,
    )
    terms = []
    for _ in range(3):
        terms.append(left.astype(BF16))
        left = left - terms[-1].astype(F32)
    result = by_transpose(jnp.concatenate(terms, axis=0), order_ref[...])
    result = (result[:96] + result[96:192]) + result[192:]
    for q in range(4):
        expand_ref[:, q * D : (q + 1) * D] = result[q * 24 : (q + 1) * 24]


def finish(pieces):
    return pl.pallas_call(
        finish_kernel,
        out_shape=(
            jax.ShapeDtypeStruct((96, D), F32),
            jax.ShapeDtypeStruct((24, FF), F32),
        ),
        in_specs=[VMEM] * 5,
        out_specs=(VMEM,) * 2,
        compiler_params=PARAMS,
        name="finish",
    )(*pieces, jnp.asarray(reorder_matrix(), BF16))


def middle(info, context_tok, own, cotangent, rows, bias, weights):
    tall = (LOCAL, D)
    return pl.pallas_call(
        middle_kernel,
        out_shape=(
            jax.ShapeDtypeStruct(tall, BF16),
            jax.ShapeDtypeStruct(tall, F32),
            jax.ShapeDtypeStruct((SP, LOCAL, HW), BF16),
            jax.ShapeDtypeStruct((8, D), F32),
            jax.ShapeDtypeStruct((4, D), F32),
            jax.ShapeDtypeStruct((D, D), BF16),
            jax.ShapeDtypeStruct((D, 2 * FF), BF16),
        ),
        in_specs=[SMEM] + [VMEM] * 5 + [pl.BlockSpec(memory_space=pl.ANY)],
        out_specs=(VMEM,) * 6 + (pl.BlockSpec(memory_space=pl.ANY),),
        scratch_shapes=[
            pltpu.VMEM((D, PACKED), BF16),
            pltpu.VMEM((D, 2 * FF), BF16),
            pltpu.VMEM((LOCAL, FF), F32),
            pltpu.VMEM((LOCAL, FF), BF16),
            pltpu.SemaphoreType.DMA((9,)),
            pltpu.SemaphoreType.DMA((8,)),
        ],
        compiler_params=pltpu.CompilerParams(vmem_limit_bytes=48 * 1024 * 1024),
        cost_estimate=pl.CostEstimate(
            flops=6 * LOCAL * D * PACKED, bytes_accessed=24 * 1024 * 1024, transcendentals=0
        ),
        name="middle",
    )(info, context_tok, own, cotangent, rows, bias, weights)


def from_x(values, x_at):
    pieces = [values] + [to_x(values, -step) for step in (1, 2, 3)]
    return rolled(jnp.stack(pieces), SP - x_at)


def per_device(
    hidden_in,
    lengths,
    qkv_weight,
    query_bias,
    value_bias,
    context_weight,
    context_bias,
    first_gain,
    first_shift,
    expand_weight,
    expand_bias,
    reduce_weight,
    reduce_bias,
    second_gain,
    second_shift,
    out_grad,
):
    x_at = lax.axis_index("sp")
    own = hidden_in[0]
    tokens = [own] + [None] * 3
    for step in ORDER:
        tokens[step] = to_x(own, -step)

    info = jnp.stack([x_at.astype(jnp.int32), lengths[0]])
    packed, early = pack(
        info, qkv_weight, context_weight, expand_weight, reduce_weight,
        (query_bias, value_bias, context_bias, first_gain, first_shift, reduce_bias,
         second_gain, second_shift, expand_bias),
    )
    packed = lax.all_gather(packed, "fsdp", axis=0, tiled=True)
    early = lax.all_to_all(early, "fsdp", split_axis=0, concat_axis=0, tiled=True)
    qkv_full = early[:, :24].reshape(D, 3 * HW)
    rows = jnp.swapaxes(early[:, 24:, :24], 0, 1).reshape(8, D).astype(F32)
    query_full, value_full = rows[0], rows[1]
    expand_add = jnp.swapaxes(early[:, 24, 128:224].reshape(32, 4, 24), 0, 1)
    expand_add = expand_add.reshape(1, FF).astype(F32)

    everyone = jnp.concatenate(tokens, axis=0)
    offsets = jnp.concatenate(
        [
            lax.dynamic_slice_in_dim(query_full, x_at * HW, HW),
            jnp.zeros((HW,), F32),
            lax.dynamic_slice_in_dim(value_full, x_at * HW, HW),
        ]
    )
    qkv = (dot(everyone, qkv_full) + offsets).astype(BF16)
    context = attend(info, qkv)

    groups = [context[:LOCAL]] + [None] * 3
    for step in ORDER:
        groups[SP - step] = to_x(context[step * LOCAL : (step + 1) * LOCAL], step)
    context_tok = jnp.stack(groups)

    hidden_out, grad_one, context_grad, row_sums, bias_sums, context_sum, packed_grads = middle(
        info, context_tok, own, out_grad[0], rows, expand_add, packed
    )
    packed_grads = lax.psum_scatter(
        packed_grads,
        "fsdp",
        scatter_dimension=0,
        axis_index_groups=[[8 * z + m for m in range(8)] for z in range(4)],
        tiled=True,
    )
    z_at = lax.axis_index("fsdp") // 8

    def rows_of(step):
        return lax.dynamic_slice_in_dim(packed_grads, (z_at + step) % 4 * 24, 24, axis=0)

    z_rows = [rows_of(step) for step in range(4)]
    z_sum = z_rows[0].astype(F32)
    for step in ORDER:
        z_sum = z_sum + to_z(z_rows[step], step).astype(F32)
    packed_grads = z_sum.astype(BF16)
    blocks = [context_grad[0]] + [None] * 3
    for step in ORDER:
        blocks[SP - step] = to_x(context_grad[step], step)
    grad_heads = jnp.concatenate(blocks, axis=0)

    qkv_grad, second_round = attend_back(
        info, qkv, grad_heads, everyone, context_sum, row_sums, bias_sums
    )

    partial = by_transpose(qkv_grad, qkv_full).astype(BF16)
    input_sum = grad_one + partial[:LOCAL].astype(F32)
    for step in ORDER:
        input_sum = input_sum + to_x(partial[step * LOCAL : (step + 1) * LOCAL], step).astype(F32)
    input_grad = input_sum.astype(BF16)[None]

    second_round = lax.all_to_all(
        second_round.reshape(32, 24, LATE),
        "fsdp",
        split_axis=0,
        concat_axis=0,
        tiled=True,
    )
    second_round = add_up(second_round, z_rows[0])
    second_round = from_x(second_round, x_at).astype(F32)
    qkv_out = jnp.transpose(second_round[:, :, D + 128 :].reshape(SP, 24, 3, HW), (1, 2, 0, 3))
    qkv_out = qkv_out.reshape(24, 3 * D)
    context_out = jnp.sum(second_round[:, :, :D], axis=0)
    eight = jnp.sum(second_round[:, :, D : D + 12], axis=0).T
    expand_bias_out = eight[8:].reshape(96)

    reduce_out, expand_out = finish(
        [packed_grads] + [to_x(packed_grads, step) for step in ORDER]
    )

    return (
        hidden_out[None],
        input_grad,
        qkv_out,
        eight[0],
        eight[1],
        context_out,
        eight[2],
        eight[3],
        eight[4],
        expand_out,
        expand_bias_out,
        reduce_out,
        eight[5],
        eight[6],
        eight[7],
    )


def solution(mesh):
    sequences = P("fsdp", "sp", None)
    matrix = P("fsdp", None)
    vector = P("fsdp")
    return jax.shard_map(
        per_device,
        mesh=mesh,
        in_specs=(
            sequences, vector, matrix, vector, vector, matrix, vector, vector, vector,
            matrix, vector, matrix, vector, vector, vector, sequences,
        ),
        out_specs=(
            sequences, sequences, matrix, vector, vector, matrix, vector, vector, vector,
            matrix, vector, matrix, vector, vector, vector,
        ),
        check_vma=False,
    )
```

```python
import jax
import jax.numpy as jnp
import numpy as np
from jax import lax
from jax.experimental import pallas as pl
from jax.experimental.pallas import tpu as pltpu
from jax.sharding import PartitionSpec as P

D = 768
H = 12
DH = 64
FF = 3072
SP = 4
LOCAL = 256
LEN = 1024
HEADS = H // SP
HW = HEADS * DH
BLOCK = 256

EPSILON = 1e-06
SCALING = 0.125
MASKED = -1000000000.0
F32 = jnp.float32
BF16 = jnp.bfloat16


def normalize(values, gain_row, shift_row):
    average = jnp.mean(values, axis=-1, keepdims=True)
    centred = values - average
    inv_std = lax.rsqrt(jnp.mean(centred * centred, axis=-1, keepdims=True) + EPSILON)
    normed = centred * inv_std
    return (normed * gain_row + shift_row, normed, inv_std)


def normalize_back(upstream, normed, inv_std, gain_row):
    weighted = upstream * gain_row
    return inv_std * (
        weighted
        - jnp.mean(weighted, axis=-1, keepdims=True)
        - normed * jnp.mean(weighted * normed, axis=-1, keepdims=True)
    )


def dot(left_side, right_side):
    return jnp.dot(left_side, right_side, preferred_element_type=F32)


def rows_first(left_side, right_side):
    return lax.dot_general(
        left_side, right_side, (((0,), (0,)), ((), ())), preferred_element_type=F32
    )


def by_transpose(left_side, right_side):
    return lax.dot_general(
        left_side, right_side, (((1,), (1,)), ((), ())), preferred_element_type=F32
    )


ROOT = 0.7978845608028654
CUBE = 0.044715


def gate_and_slope(values):
    square = values * values
    bent = jnp.tanh(ROOT * values * (1.0 + CUBE * square))
    half = 0.5 * (1.0 + bent)
    slope = half + 0.5 * values * (1.0 - bent * bent) * (ROOT * (1.0 + 3.0 * CUBE * square))
    return values * half, slope


def to_x(values, step):
    return lax.ppermute(values, "sp", [(i, (i + step) % SP) for i in range(SP)])


def to_core(values):
    return lax.ppermute(values, "fsdp", [(i, i ^ 1) for i in range(32)])


def to_z(values, step):
    return lax.ppermute(values, "fsdp", [(i, (i + 8 * step) % 32) for i in range(32)])


ORDER = (1, 3, 2)


def rolled(values, start):
    count = values.shape[0]
    return lax.dynamic_slice_in_dim(
        jnp.concatenate([values, values], axis=0), start % count, count, axis=0
    )


def masked_keys(info_ref, shape, dim):
    at = lax.broadcasted_iota(jnp.int32, shape, dim)
    block = (info_ref[0] + lax.shift_right_logical(at, 8)) & 3
    return (block * LOCAL + (at & (LOCAL - 1))) < info_ref[1]


def attend_kernel(info_ref, qkv_ref, context_ref):
    valid = masked_keys(info_ref, (1, LEN), 1)

    @pl.loop(0, LEN // BLOCK)
    def _(step):
        rows = pl.ds(pl.multiple_of(step * BLOCK, BLOCK), BLOCK)
        outs = []
        for head in range(HEADS):
            cols = head * DH
            keys = qkv_ref[:, HW + cols : HW + cols + DH]
            vals = qkv_ref[:, 2 * HW + cols : 2 * HW + cols + DH]
            queries = qkv_ref[rows, cols : cols + DH] * jnp.asarray(SCALING, BF16)
            scores = jnp.where(valid, by_transpose(queries, keys), MASKED)
            weights = jnp.exp(scores - jnp.max(scores, axis=-1, keepdims=True))
            totals = jnp.sum(weights, axis=-1, keepdims=True)
            outs.append(dot(weights.astype(BF16), vals) * (1.0 / totals))
        context_ref[rows, :] = jnp.concatenate(outs, axis=1).astype(BF16)


def attend_back_kernel(
    info_ref, qkv_ref, grad_ref, tokens_ref, sums_ref, bias_sum_ref,
    out_ref, mine_ref, other_ref, key_sum, value_sum, stack,
):
    valid = masked_keys(info_ref, (LEN, 1), 0)
    key_sum[...] = jnp.zeros_like(key_sum)
    value_sum[...] = jnp.zeros_like(value_sum)

    @pl.loop(0, LEN // BLOCK)
    def _(step):
        rows = pl.ds(pl.multiple_of(step * BLOCK, BLOCK), BLOCK)
        outs = []
        for head in range(HEADS):
            cols = head * DH
            keys = qkv_ref[:, HW + cols : HW + cols + DH]
            vals = qkv_ref[:, 2 * HW + cols : 2 * HW + cols + DH]
            queries = qkv_ref[rows, cols : cols + DH] * jnp.asarray(SCALING, BF16)
            grads = grad_ref[rows, cols : cols + DH]
            scores = jnp.where(valid, by_transpose(keys, queries), MASKED)
            weights = jnp.exp(scores - jnp.max(scores, axis=0, keepdims=True))
            probs = weights * (1.0 / jnp.sum(weights, axis=0, keepdims=True))
            value_sum[head] += dot(probs.astype(BF16), grads)
            prob_grad = by_transpose(vals, grads)
            centre = jnp.sum(probs * prob_grad, axis=0, keepdims=True)
            score_grad = (probs * (prob_grad - centre)).astype(BF16)
            key_sum[head] += dot(score_grad, queries)
            outs.append(rows_first(score_grad, keys) * SCALING)
        out_ref[rows, :HW] = jnp.concatenate(outs, axis=1).astype(BF16)

    for part, total in ((1, key_sum), (2, value_sum)):
        out_ref[:, part * HW : (part + 1) * HW] = jnp.concatenate(
            [total[head] for head in range(HEADS)], axis=1
        ).astype(BF16)

    low = out_ref[...]
    sums = jnp.sum(low.astype(F32), axis=0, keepdims=True)
    stack[...] = jnp.zeros_like(stack)
    for row, part in ((0, 0), (1, 2)):
        own = sums[:, part * HW : (part + 1) * HW]
        stack[row : row + 1, :] = jnp.concatenate(
            [jnp.where(info_ref[0] == at, own, 0.0) for at in range(SP)], axis=1
        )
    stack[2:8, :] = sums_ref[0:6, :]
    stack[8:12, :] = bias_sum_ref[...]
    mine_ref[:, 128 + 3 * HW :] = jnp.zeros((D // 2, LATE - 128 - 3 * HW), BF16)
    other_ref[:, 128 + 3 * HW :] = jnp.zeros((D // 2, LATE - 128 - 3 * HW), BF16)
    for cols, full in (
        (slice(0, 128), stack[...].T),
        (slice(128, 128 + 3 * HW), rows_first(tokens_ref[...], low)),
    ):
        even, odd = (
            jnp.concatenate(
                [full[(2 * chip + at) * 24 : (2 * chip + at + 1) * 24] for chip in range(16)], axis=0
            )
            for at in range(2)
        )
        first = info_ref[2] == 0
        mine_ref[:, cols] = jnp.where(first, even, odd).astype(BF16)
        other_ref[:, cols] = jnp.where(first, odd, even).astype(BF16)


PACKED = 2 * FF + D
LATE = D


def reorder_matrix():
    source = np.arange(D).reshape(8, 4, 24).transpose(1, 0, 2).reshape(D)
    matrix = np.zeros((D, D), np.float32)
    matrix[source, np.arange(D)] = 1.0
    return matrix


def pack_kernel(info_ref, *rest):
    sources, (packed_ref, early_ref), held = rest[:14], rest[14:16], rest[16:30]
    rows_ref, sems = rest[30:]
    fetches = [
        pltpu.make_async_copy(source, target, sems.at[at])
        for at, (source, target) in enumerate(zip(sources, held))
    ]
    for fetch in fetches:
        fetch.start()
    qkv_ref, context_ref, expand_ref, reduce_ref, order_ref = held[:5]
    vector_refs = held[5:]
    for fetch in fetches:
        fetch.wait()
    reduce_rows = reduce_ref[...].astype(F32)
    for part in range(4):
        packed_ref[:, part * D : (part + 1) * D] = reduce_rows[part * 24 : (part + 1) * 24].astype(BF16)
    stacked = jnp.concatenate(
        [expand_ref[:, q * D : (q + 1) * D].astype(F32) for q in range(4)], axis=0
    )
    stacked = dot(stacked.astype(BF16), order_ref[...])
    moved = [stacked[q * 24 : (q + 1) * 24] for q in range(4)]
    for part in range(4):
        packed_ref[:, FF + part * D : FF + (part + 1) * D] = jnp.concatenate(
            [values[:, part * HW : (part + 1) * HW] for values in moved], axis=1
        ).astype(BF16)
    packed_ref[:, 2 * FF :] = context_ref[...]

    rows_ref[...] = jnp.zeros_like(rows_ref)
    for row in range(8):
        rows_ref[row : row + 1, :24] = vector_refs[row][...].astype(F32).reshape(1, 24)
    rows_ref[0:1, 128:224] = vector_refs[8][...].astype(F32).reshape(1, 96)
    for at in range(SP):

        @pl.when(info_ref[0] == at)
        def _(at=at):
            own = jnp.concatenate(
                [qkv_ref[:, part * D + at * HW : part * D + (at + 1) * HW] for part in range(3)],
                axis=1,
            )
            block = jnp.concatenate([own.astype(F32), rows_ref[...]], axis=0).astype(BF16)

            @pl.loop(0, 32)
            def _(owner):
                early_ref[owner] = block


def middle_kernel(
    info_ref, context_ref, own_ref, cotangent_ref, rows_ref, bias_ref, weights_ref,
    hidden_ref, grad_one_ref, context_grad_ref, sums_ref, bias_sum_ref, grads_ref,
    held, made, slopes, active, in_sems, out_sems,
):
    def piece(block):
        return slice(block * D, (block + 1) * D)

    copies = {}
    for block in (8, 4, 0, 5, 1, 6, 2, 7, 3):
        copies[block] = pltpu.make_async_copy(
            weights_ref.at[:, piece(block)], held.at[:, piece(block)], in_sems.at[block]
        )
        copies[block].start()

    def send(block):
        copy = pltpu.make_async_copy(
            made.at[:, piece(block)], grads_ref.at[:, piece(block)], out_sems.at[block]
        )
        copy.start()
        return copy

    context_add, gain_one, shift_one, reduce_add, gain_two, shift_two = (
        rows_ref[row : row + 1, :] for row in range(2, 8)
    )
    groups = [(z - info_ref[0]) & 3 for z in range(SP)]

    def by_plane(values):
        return jnp.concatenate(
            [values[(8 * z + m) * 24 : (8 * z + m + 1) * 24] for m in range(8) for z in range(4)],
            axis=0,
        ).astype(BF16)

    own = own_ref[...].astype(F32) + context_add
    copies[8].wait()
    for block in range(SP):
        own = own + dot(
            context_ref[groups[block]], held[block * HW : (block + 1) * HW, piece(8)]
        )
    first_out, normed_one, inv_one = normalize(own, gain_one, shift_one)
    first_low = first_out.astype(BF16)
    second_in = first_out + reduce_add
    for part in range(4):
        copies[4 + part].wait()
        expand = dot(first_low, held[:, piece(4 + part)]) + bias_ref[:, piece(part)]
        value, slope = gate_and_slope(expand)
        active[:, piece(part)] = value.astype(BF16)
        slopes[:, piece(part)] = slope
        copies[part].wait()
        second_in = second_in + dot(active[:, piece(part)], held[:, piece(part)])
    second_out, normed_two, inv_two = normalize(second_in, gain_two, shift_two)
    hidden_ref[...] = second_out.astype(BF16)

    cotangent = cotangent_ref[...].astype(F32)
    grad_two = normalize_back(cotangent, normed_two, inv_two, gain_two)
    reduced_grad = grad_two.astype(BF16)
    sums_ref[...] = jnp.zeros_like(sums_ref)
    sums_ref[3:4, :] = jnp.sum(reduced_grad.astype(F32), axis=0, keepdims=True)
    sums_ref[4:5, :] = jnp.sum(cotangent * normed_two, axis=0, keepdims=True)
    sums_ref[5:6, :] = jnp.sum(cotangent, axis=0, keepdims=True)
    first_grad = grad_two
    sent = []
    for part in range(4):
        active_grad = by_transpose(reduced_grad, held[:, piece(part)]).astype(BF16)
        expand_grad = (active_grad.astype(F32) * slopes[:, piece(part)]).astype(BF16)
        bias_sum_ref[part : part + 1, :] = jnp.sum(expand_grad.astype(F32), axis=0, keepdims=True)
        first_grad = first_grad + by_transpose(expand_grad, held[:, piece(4 + part)])
        made[:, piece(part)] = by_plane(rows_first(active[:, piece(part)], reduced_grad))
        sent.append(send(part))
        made[:, piece(4 + part)] = by_plane(rows_first(first_low, expand_grad))
        sent.append(send(4 + part))
    sums_ref[1:2, :] = jnp.sum(first_grad * normed_one, axis=0, keepdims=True)
    sums_ref[2:3, :] = jnp.sum(first_grad, axis=0, keepdims=True)
    grad_one = normalize_back(first_grad, normed_one, inv_one, gain_one)
    grad_one_ref[...] = grad_one
    branch_grad = grad_one.astype(BF16)
    sums_ref[0:1, :] = jnp.sum(branch_grad.astype(F32), axis=0, keepdims=True)
    made[:, piece(8)] = by_plane(
        jnp.concatenate([rows_first(context_ref[group], branch_grad) for group in groups], axis=0)
    )
    sent.append(send(8))
    for block in range(SP):
        context_grad_ref[groups[block]] = by_transpose(
            branch_grad, held[block * HW : (block + 1) * HW, piece(8)]
        ).astype(BF16)
    for copy in sent:
        copy.wait()


SMEM = pl.BlockSpec(memory_space=pltpu.SMEM)
VMEM = pl.BlockSpec(memory_space=pltpu.VMEM)
PARAMS = pltpu.CompilerParams(vmem_limit_bytes=40 * 1024 * 1024)


def attend(info, qkv):
    return pl.pallas_call(
        attend_kernel,
        out_shape=jax.ShapeDtypeStruct((LEN, HW), BF16),
        in_specs=[SMEM, VMEM],
        out_specs=VMEM,
        compiler_params=PARAMS,
        cost_estimate=pl.CostEstimate(
            flops=4 * HEADS * LEN * LEN * 256, bytes_accessed=LEN * HW * 8, transcendentals=0
        ),
        name="attend",
    )(info, qkv)


def attend_back(info, qkv, grads, tokens, row_sums, bias_sums):
    return pl.pallas_call(
        attend_back_kernel,
        out_shape=(
            jax.ShapeDtypeStruct((LEN, 3 * HW), BF16),
            jax.ShapeDtypeStruct((D // 2, LATE), BF16),
            jax.ShapeDtypeStruct((D // 2, LATE), BF16),
        ),
        in_specs=[SMEM] + [VMEM] * 5,
        out_specs=(VMEM,) * 3,
        scratch_shapes=[
            pltpu.VMEM((HEADS, LEN, DH), F32),
            pltpu.VMEM((HEADS, LEN, DH), F32),
            pltpu.VMEM((128, D), F32),
        ],
        compiler_params=PARAMS,
        cost_estimate=pl.CostEstimate(
            flops=10 * HEADS * LEN * LEN * 256, bytes_accessed=LEN * HW * 14, transcendentals=0
        ),
        name="attend_back",
    )(info, qkv, grads, tokens, row_sums, bias_sums)


def pack(info, qkv_weight, context_weight, expand_weight, reduce_weight, vectors):
    operands = (
        qkv_weight, context_weight, expand_weight, reduce_weight,
        jnp.asarray(reorder_matrix(), BF16), *vectors,
    )
    return pl.pallas_call(
        pack_kernel,
        out_shape=(
            jax.ShapeDtypeStruct((24, PACKED), BF16),
            jax.ShapeDtypeStruct((32, 32, 3 * HW), BF16),
        ),
        in_specs=[SMEM] + [pl.BlockSpec(memory_space=pltpu.HBM)] * len(operands),
        out_specs=(VMEM, VMEM),
        scratch_shapes=[pltpu.VMEM(operand.shape, BF16) for operand in operands]
        + [pltpu.VMEM((8, 3 * HW), F32), pltpu.SemaphoreType.DMA((len(operands),))],
        compiler_params=pltpu.CompilerParams(vmem_limit_bytes=60 * 1024 * 1024),
        name="pack",
    )(info, *operands)


def finish_kernel(a_ref, b_ref, c_ref, d_ref, order_ref, reduce_ref, expand_ref, context_ref):
    def total(start, width):
        parts = [ref[:, start : start + width].astype(F32) for ref in (a_ref, b_ref, c_ref, d_ref)]
        return (parts[0] + parts[1]) + (parts[2] + parts[3])

    for part in range(4):
        reduce_ref[part * 24 : (part + 1) * 24, :] = total(part * D, D)
    context_ref[...] = total(2 * FF, D)
    moved = [total(FF + part * D, D) for part in range(4)]
    left = jnp.concatenate(
        [
            jnp.concatenate([values[:, q * HW : (q + 1) * HW] for values in moved], axis=1)
            for q in range(4)
        ],
        axis=0,
    )
    terms = []
    for _ in range(3):
        terms.append(left.astype(BF16))
        left = left - terms[-1].astype(F32)
    result = by_transpose(jnp.concatenate(terms, axis=0), order_ref[...])
    result = (result[:96] + result[96:192]) + result[192:]
    for q in range(4):
        expand_ref[:, q * D : (q + 1) * D] = result[q * 24 : (q + 1) * 24]


def finish(pieces):
    return pl.pallas_call(
        finish_kernel,
        out_shape=(
            jax.ShapeDtypeStruct((96, D), F32),
            jax.ShapeDtypeStruct((24, FF), F32),
            jax.ShapeDtypeStruct((24, D), F32),
        ),
        in_specs=[VMEM] * 5,
        out_specs=(VMEM,) * 3,
        compiler_params=PARAMS,
        name="finish",
    )(*pieces, jnp.asarray(reorder_matrix(), BF16))


def middle(info, context_tok, own, cotangent, rows, bias, weights):
    tall = (LOCAL, D)
    return pl.pallas_call(
        middle_kernel,
        out_shape=(
            jax.ShapeDtypeStruct(tall, BF16),
            jax.ShapeDtypeStruct(tall, F32),
            jax.ShapeDtypeStruct((SP, LOCAL, HW), BF16),
            jax.ShapeDtypeStruct((8, D), F32),
            jax.ShapeDtypeStruct((4, D), F32),
            jax.ShapeDtypeStruct((D, PACKED), BF16),
        ),
        in_specs=[SMEM] + [VMEM] * 5 + [pl.BlockSpec(memory_space=pl.ANY)],
        out_specs=(VMEM,) * 5 + (pl.BlockSpec(memory_space=pl.ANY),),
        scratch_shapes=[
            pltpu.VMEM((D, PACKED), BF16),
            pltpu.VMEM((D, PACKED), BF16),
            pltpu.VMEM((LOCAL, FF), F32),
            pltpu.VMEM((LOCAL, FF), BF16),
            pltpu.SemaphoreType.DMA((9,)),
            pltpu.SemaphoreType.DMA((9,)),
        ],
        compiler_params=pltpu.CompilerParams(vmem_limit_bytes=48 * 1024 * 1024),
        cost_estimate=pl.CostEstimate(
            flops=6 * LOCAL * D * PACKED, bytes_accessed=24 * 1024 * 1024, transcendentals=0
        ),
        name="middle",
    )(info, context_tok, own, cotangent, rows, bias, weights)


def from_x(values, x_at):
    pieces = [values] + [to_x(values, -step) for step in (1, 2, 3)]
    return rolled(jnp.stack(pieces), SP - x_at)


def per_device(
    hidden_in,
    lengths,
    qkv_weight,
    query_bias,
    value_bias,
    context_weight,
    context_bias,
    first_gain,
    first_shift,
    expand_weight,
    expand_bias,
    reduce_weight,
    reduce_bias,
    second_gain,
    second_shift,
    out_grad,
):
    x_at = lax.axis_index("sp")
    own = hidden_in[0]
    tokens = [own] + [None] * 3
    for step in ORDER:
        tokens[step] = to_x(own, -step)

    core = lax.axis_index("fsdp") & 1
    info = jnp.stack([x_at.astype(jnp.int32), lengths[0], core.astype(jnp.int32)])
    packed, early = pack(
        info, qkv_weight, context_weight, expand_weight, reduce_weight,
        (query_bias, value_bias, context_bias, first_gain, first_shift, reduce_bias,
         second_gain, second_shift, expand_bias),
    )
    packed = lax.all_gather(packed, "fsdp", axis=0, tiled=True)
    early = lax.all_to_all(early, "fsdp", split_axis=0, concat_axis=0, tiled=True)
    qkv_full = early[:, :24].reshape(D, 3 * HW)
    rows = jnp.swapaxes(early[:, 24:, :24], 0, 1).reshape(8, D).astype(F32)
    query_full, value_full = rows[0], rows[1]
    expand_add = jnp.swapaxes(early[:, 24, 128:224].reshape(32, 4, 24), 0, 1)
    expand_add = expand_add.reshape(1, FF).astype(F32)

    everyone = jnp.concatenate(tokens, axis=0)
    offsets = jnp.concatenate(
        [
            lax.dynamic_slice_in_dim(query_full, x_at * HW, HW),
            jnp.zeros((HW,), F32),
            lax.dynamic_slice_in_dim(value_full, x_at * HW, HW),
        ]
    )
    qkv = (dot(everyone, qkv_full) + offsets).astype(BF16)
    context = attend(info, qkv)

    groups = [context[:LOCAL]] + [None] * 3
    for step in ORDER:
        groups[SP - step] = to_x(context[step * LOCAL : (step + 1) * LOCAL], step)
    context_tok = jnp.stack(groups)

    hidden_out, grad_one, context_grad, row_sums, bias_sums, packed_grads = middle(
        info, context_tok, own, out_grad[0], rows, expand_add, packed
    )
    packed_grads = lax.psum_scatter(
        packed_grads,
        "fsdp",
        scatter_dimension=0,
        axis_index_groups=[[8 * z + m for m in range(8)] for z in range(4)],
        tiled=True,
    )
    z_at = lax.axis_index("fsdp") // 8

    def rows_of(step):
        return lax.dynamic_slice_in_dim(packed_grads, (z_at + step) % 4 * 24, 24, axis=0)

    z_sum = rows_of(0).astype(F32)
    for step in ORDER:
        z_sum = z_sum + to_z(rows_of(step), step).astype(F32)
    packed_grads = z_sum.astype(BF16)
    blocks = [context_grad[0]] + [None] * 3
    for step in ORDER:
        blocks[SP - step] = to_x(context_grad[step], step)
    grad_heads = jnp.concatenate(blocks, axis=0)

    qkv_grad, mine, other = attend_back(info, qkv, grad_heads, everyone, row_sums, bias_sums)
    second_round = (mine.astype(F32) + to_core(other).astype(F32)).astype(BF16)

    partial = by_transpose(qkv_grad, qkv_full).astype(BF16)
    input_sum = grad_one + partial[:LOCAL].astype(F32)
    for step in ORDER:
        input_sum = input_sum + to_x(partial[step * LOCAL : (step + 1) * LOCAL], step).astype(F32)
    input_grad = input_sum.astype(BF16)[None]

    second_round = lax.all_to_all(
        second_round.reshape(16, 24, LATE),
        "fsdp",
        split_axis=0,
        concat_axis=0,
        axis_index_groups=[[2 * chip + at for chip in range(16)] for at in range(2)],
        tiled=True,
    )
    second_round = jnp.sum(second_round.astype(F32), axis=0).astype(BF16)
    second_round = from_x(second_round, x_at).astype(F32)
    qkv_out = jnp.transpose(second_round[:, :, 128 : 128 + 3 * HW].reshape(SP, 24, 3, HW), (1, 2, 0, 3))
    qkv_out = qkv_out.reshape(24, 3 * D)
    eight = jnp.sum(second_round[:, :, :12], axis=0).T
    expand_bias_out = eight[8:].reshape(96)

    reduce_out, expand_out, context_out = finish(
        [packed_grads] + [to_x(packed_grads, step) for step in ORDER]
    )

    return (
        hidden_out[None],
        input_grad,
        qkv_out,
        eight[0],
        eight[1],
        context_out,
        eight[2],
        eight[3],
        eight[4],
        expand_out,
        expand_bias_out,
        reduce_out,
        eight[5],
        eight[6],
        eight[7],
    )


def solution(mesh):
    sequences = P("fsdp", "sp", None)
    matrix = P("fsdp", None)
    vector = P("fsdp")
    return jax.shard_map(
        per_device,
        mesh=mesh,
        in_specs=(
            sequences, vector, matrix, vector, vector, matrix, vector, vector, vector,
            matrix, vector, matrix, vector, vector, vector, sequences,
        ),
        out_specs=(
            sequences, sequences, matrix, vector, vector, matrix, vector, vector, vector,
            matrix, vector, matrix, vector, vector, vector,
        ),
        check_vma=False,
    )
```

```python
import jax
import jax.numpy as jnp
import numpy as np
from jax import lax
from jax.experimental import pallas as pl
from jax.experimental.pallas import tpu as pltpu
from jax.sharding import PartitionSpec as P

D = 768
H = 12
DH = 64
FF = 3072
SP = 4
LOCAL = 256
LEN = 1024
HEADS = H // SP
HW = HEADS * DH
BLOCK = 256

EPSILON = 1e-06
SCALING = 0.125
MASKED = -1000000000.0
F32 = jnp.float32
BF16 = jnp.bfloat16


def normalize(values, gain_row, shift_row):
    average = jnp.mean(values, axis=-1, keepdims=True)
    centred = values - average
    inv_std = lax.rsqrt(jnp.mean(centred * centred, axis=-1, keepdims=True) + EPSILON)
    normed = centred * inv_std
    return (normed * gain_row + shift_row, normed, inv_std)


def normalize_back(upstream, normed, inv_std, gain_row):
    weighted = upstream * gain_row
    return inv_std * (
        weighted
        - jnp.mean(weighted, axis=-1, keepdims=True)
        - normed * jnp.mean(weighted * normed, axis=-1, keepdims=True)
    )


def dot(left_side, right_side):
    return jnp.dot(left_side, right_side, preferred_element_type=F32)


def rows_first(left_side, right_side):
    return lax.dot_general(
        left_side, right_side, (((0,), (0,)), ((), ())), preferred_element_type=F32
    )


def by_transpose(left_side, right_side):
    return lax.dot_general(
        left_side, right_side, (((1,), (1,)), ((), ())), preferred_element_type=F32
    )


ROOT = 0.7978845608028654
CUBE = 0.044715


def gate_and_slope(values):
    square = values * values
    bent = jnp.tanh(ROOT * values * (1.0 + CUBE * square))
    half = 0.5 * (1.0 + bent)
    slope = half + 0.5 * values * (1.0 - bent * bent) * (ROOT * (1.0 + 3.0 * CUBE * square))
    return values * half, slope


def to_x(values, step):
    return lax.ppermute(values, "sp", [(i, (i + step) % SP) for i in range(SP)])


def to_core(values):
    return lax.ppermute(values, "fsdp", [(i, i ^ 1) for i in range(32)])


def to_z(values, step):
    return lax.ppermute(values, "fsdp", [(i, (i + 8 * step) % 32) for i in range(32)])


ORDER = (1, 3, 2)


def rolled(values, start):
    count = values.shape[0]
    return lax.dynamic_slice_in_dim(
        jnp.concatenate([values, values], axis=0), start % count, count, axis=0
    )


def masked_keys(info_ref, shape, dim):
    at = lax.broadcasted_iota(jnp.int32, shape, dim)
    block = (info_ref[0] + lax.shift_right_logical(at, 8)) & 3
    return (block * LOCAL + (at & (LOCAL - 1))) < info_ref[1]


def attend_kernel(info_ref, qkv_ref, context_ref):
    valid = masked_keys(info_ref, (1, LEN), 1)

    @pl.loop(0, LEN // BLOCK)
    def _(step):
        rows = pl.ds(pl.multiple_of(step * BLOCK, BLOCK), BLOCK)
        outs = []
        for head in range(HEADS):
            cols = head * DH
            keys = qkv_ref[:, HW + cols : HW + cols + DH]
            vals = qkv_ref[:, 2 * HW + cols : 2 * HW + cols + DH]
            queries = qkv_ref[rows, cols : cols + DH] * jnp.asarray(SCALING, BF16)
            scores = jnp.where(valid, by_transpose(queries, keys), MASKED)
            weights = jnp.exp(scores - jnp.max(scores, axis=-1, keepdims=True))
            totals = jnp.sum(weights, axis=-1, keepdims=True)
            outs.append(dot(weights.astype(BF16), vals) * (1.0 / totals))
        context_ref[rows, :] = jnp.concatenate(outs, axis=1).astype(BF16)


def attend_back_kernel(
    info_ref, qkv_ref, grad_ref, tokens_ref, sums_ref, bias_sum_ref,
    out_ref, mine_ref, other_ref, key_sum, value_sum, stack,
):
    valid = masked_keys(info_ref, (LEN, 1), 0)
    key_sum[...] = jnp.zeros_like(key_sum)
    value_sum[...] = jnp.zeros_like(value_sum)

    @pl.loop(0, LEN // BLOCK)
    def _(step):
        rows = pl.ds(pl.multiple_of(step * BLOCK, BLOCK), BLOCK)
        outs = []
        for head in range(HEADS):
            cols = head * DH
            keys = qkv_ref[:, HW + cols : HW + cols + DH]
            vals = qkv_ref[:, 2 * HW + cols : 2 * HW + cols + DH]
            queries = qkv_ref[rows, cols : cols + DH] * jnp.asarray(SCALING, BF16)
            grads = grad_ref[rows, cols : cols + DH]
            scores = jnp.where(valid, by_transpose(keys, queries), MASKED)
            weights = jnp.exp(scores - jnp.max(scores, axis=0, keepdims=True))
            probs = weights * (1.0 / jnp.sum(weights, axis=0, keepdims=True))
            value_sum[head] += dot(probs.astype(BF16), grads)
            prob_grad = by_transpose(vals, grads)
            centre = jnp.sum(probs * prob_grad, axis=0, keepdims=True)
            score_grad = (probs * (prob_grad - centre)).astype(BF16)
            key_sum[head] += dot(score_grad, queries)
            outs.append(rows_first(score_grad, keys) * SCALING)
        out_ref[rows, :HW] = jnp.concatenate(outs, axis=1).astype(BF16)

    for part, total in ((1, key_sum), (2, value_sum)):
        out_ref[:, part * HW : (part + 1) * HW] = jnp.concatenate(
            [total[head] for head in range(HEADS)], axis=1
        ).astype(BF16)

    low = out_ref[...]
    sums = jnp.sum(low.astype(F32), axis=0, keepdims=True)
    stack[...] = jnp.zeros_like(stack)
    for row, part in ((0, 0), (1, 2)):
        own = sums[:, part * HW : (part + 1) * HW]
        stack[row : row + 1, :] = jnp.concatenate(
            [jnp.where(info_ref[0] == at, own, 0.0) for at in range(SP)], axis=1
        )
    stack[2:8, :] = sums_ref[0:6, :]
    stack[8:12, :] = bias_sum_ref[...]
    mine_ref[:, 128 + 3 * HW :] = jnp.zeros((D // 2, LATE - 128 - 3 * HW), BF16)
    other_ref[:, 128 + 3 * HW :] = jnp.zeros((D // 2, LATE - 128 - 3 * HW), BF16)
    for cols, full in (
        (slice(0, 128), stack[...].T),
        (slice(128, 128 + 3 * HW), rows_first(tokens_ref[...], low)),
    ):
        even, odd = (
            jnp.concatenate(
                [full[(2 * chip + at) * 24 : (2 * chip + at + 1) * 24] for chip in range(16)], axis=0
            )
            for at in range(2)
        )
        first = info_ref[2] == 0
        mine_ref[:, cols] = jnp.where(first, even, odd).astype(BF16)
        other_ref[:, cols] = jnp.where(first, odd, even).astype(BF16)


PACKED = 2 * FF + D
LATE = D


def reorder_matrix():
    source = np.arange(D).reshape(8, 4, 24).transpose(1, 0, 2).reshape(D)
    matrix = np.zeros((D, D), np.float32)
    matrix[source, np.arange(D)] = 1.0
    return matrix


def fetch(sources, held, sems):
    copies = [
        pltpu.make_async_copy(source, target, sems.at[at])
        for at, (source, target) in enumerate(zip(sources, held))
    ]
    for copy in copies:
        copy.start()
    for copy in copies:
        copy.wait()


def pack_kernel(*refs):
    packed_ref, held, sems = refs[4], refs[5:9], refs[9]
    fetch(refs[:4], held, sems)
    context_ref, expand_ref, reduce_ref, order_ref = held
    reduce_rows = reduce_ref[...].astype(F32)
    for part in range(4):
        packed_ref[:, part * D : (part + 1) * D] = reduce_rows[part * 24 : (part + 1) * 24].astype(BF16)
    stacked = jnp.concatenate(
        [expand_ref[:, q * D : (q + 1) * D].astype(F32) for q in range(4)], axis=0
    )
    stacked = dot(stacked.astype(BF16), order_ref[...])
    moved = [stacked[q * 24 : (q + 1) * 24] for q in range(4)]
    for part in range(4):
        packed_ref[:, FF + part * D : FF + (part + 1) * D] = jnp.concatenate(
            [values[:, part * HW : (part + 1) * HW] for values in moved], axis=1
        ).astype(BF16)
    packed_ref[:, 2 * FF :] = context_ref[...]


def early_kernel(info_ref, after_ref, *refs):
    early_ref, held, (rows_ref, sems) = refs[10], refs[11:21], refs[21:]
    fetch(refs[:10], held, sems)
    qkv_ref, vector_refs = held[0], held[1:]
    rows_ref[...] = jnp.zeros_like(rows_ref)
    for row in range(8):
        rows_ref[row : row + 1, :24] = vector_refs[row][...].astype(F32).reshape(1, 24)
    rows_ref[0:1, 128:224] = vector_refs[8][...].astype(F32).reshape(1, 96)
    for at in range(SP):

        @pl.when(info_ref[0] == at)
        def _(at=at):
            own = jnp.concatenate(
                [qkv_ref[:, part * D + at * HW : part * D + (at + 1) * HW] for part in range(3)],
                axis=1,
            )
            block = jnp.concatenate([own.astype(F32), rows_ref[...]], axis=0).astype(BF16)

            @pl.loop(0, 32)
            def _(owner):
                early_ref[owner] = block


def middle_kernel(
    info_ref, context_ref, own_ref, cotangent_ref, rows_ref, bias_ref, weights_ref,
    hidden_ref, grad_one_ref, context_grad_ref, sums_ref, bias_sum_ref, grads_ref,
    held, made, slopes, active, in_sems, out_sems,
):
    def piece(block):
        return slice(block * D, (block + 1) * D)

    copies = {}
    for block in (8, 4, 0, 5, 1, 6, 2, 7, 3):
        copies[block] = pltpu.make_async_copy(
            weights_ref.at[:, piece(block)], held.at[:, piece(block)], in_sems.at[block]
        )
        copies[block].start()

    def send(block):
        copy = pltpu.make_async_copy(
            made.at[:, piece(block)], grads_ref.at[:, piece(block)], out_sems.at[block]
        )
        copy.start()
        return copy

    context_add, gain_one, shift_one, reduce_add, gain_two, shift_two = (
        rows_ref[row : row + 1, :] for row in range(2, 8)
    )
    groups = [(z - info_ref[0]) & 3 for z in range(SP)]

    def by_plane(values):
        return jnp.concatenate(
            [values[(8 * z + m) * 24 : (8 * z + m + 1) * 24] for m in range(8) for z in range(4)],
            axis=0,
        ).astype(BF16)

    own = own_ref[...].astype(F32) + context_add
    copies[8].wait()
    for block in range(SP):
        own = own + dot(
            context_ref[groups[block]], held[block * HW : (block + 1) * HW, piece(8)]
        )
    first_out, normed_one, inv_one = normalize(own, gain_one, shift_one)
    first_low = first_out.astype(BF16)
    second_in = first_out + reduce_add
    for part in range(4):
        copies[4 + part].wait()
        expand = dot(first_low, held[:, piece(4 + part)]) + bias_ref[:, piece(part)]
        value, slope = gate_and_slope(expand)
        active[:, piece(part)] = value.astype(BF16)
        slopes[:, piece(part)] = slope
        copies[part].wait()
        second_in = second_in + dot(active[:, piece(part)], held[:, piece(part)])
    second_out, normed_two, inv_two = normalize(second_in, gain_two, shift_two)
    hidden_ref[...] = second_out.astype(BF16)

    cotangent = cotangent_ref[...].astype(F32)
    grad_two = normalize_back(cotangent, normed_two, inv_two, gain_two)
    reduced_grad = grad_two.astype(BF16)
    sums_ref[...] = jnp.zeros_like(sums_ref)
    sums_ref[3:4, :] = jnp.sum(reduced_grad.astype(F32), axis=0, keepdims=True)
    sums_ref[4:5, :] = jnp.sum(cotangent * normed_two, axis=0, keepdims=True)
    sums_ref[5:6, :] = jnp.sum(cotangent, axis=0, keepdims=True)
    first_grad = grad_two
    sent = []
    for part in range(4):
        active_grad = by_transpose(reduced_grad, held[:, piece(part)]).astype(BF16)
        expand_grad = (active_grad.astype(F32) * slopes[:, piece(part)]).astype(BF16)
        bias_sum_ref[part : part + 1, :] = jnp.sum(expand_grad.astype(F32), axis=0, keepdims=True)
        first_grad = first_grad + by_transpose(expand_grad, held[:, piece(4 + part)])
        made[:, piece(part)] = by_plane(rows_first(active[:, piece(part)], reduced_grad))
        sent.append(send(part))
        made[:, piece(4 + part)] = by_plane(rows_first(first_low, expand_grad))
        sent.append(send(4 + part))
    sums_ref[1:2, :] = jnp.sum(first_grad * normed_one, axis=0, keepdims=True)
    sums_ref[2:3, :] = jnp.sum(first_grad, axis=0, keepdims=True)
    grad_one = normalize_back(first_grad, normed_one, inv_one, gain_one)
    grad_one_ref[...] = grad_one
    branch_grad = grad_one.astype(BF16)
    sums_ref[0:1, :] = jnp.sum(branch_grad.astype(F32), axis=0, keepdims=True)
    made[:, piece(8)] = by_plane(
        jnp.concatenate([rows_first(context_ref[group], branch_grad) for group in groups], axis=0)
    )
    sent.append(send(8))
    for block in range(SP):
        context_grad_ref[groups[block]] = by_transpose(
            branch_grad, held[block * HW : (block + 1) * HW, piece(8)]
        ).astype(BF16)
    for copy in sent:
        copy.wait()


SMEM = pl.BlockSpec(memory_space=pltpu.SMEM)
VMEM = pl.BlockSpec(memory_space=pltpu.VMEM)
PARAMS = pltpu.CompilerParams(vmem_limit_bytes=40 * 1024 * 1024)


def attend(info, qkv):
    return pl.pallas_call(
        attend_kernel,
        out_shape=jax.ShapeDtypeStruct((LEN, HW), BF16),
        in_specs=[SMEM, VMEM],
        out_specs=VMEM,
        compiler_params=PARAMS,
        cost_estimate=pl.CostEstimate(
            flops=4 * HEADS * LEN * LEN * 256, bytes_accessed=LEN * HW * 8, transcendentals=0
        ),
        name="attend",
    )(info, qkv)


def attend_back(info, qkv, grads, tokens, row_sums, bias_sums):
    return pl.pallas_call(
        attend_back_kernel,
        out_shape=(
            jax.ShapeDtypeStruct((LEN, 3 * HW), BF16),
            jax.ShapeDtypeStruct((D // 2, LATE), BF16),
            jax.ShapeDtypeStruct((D // 2, LATE), BF16),
        ),
        in_specs=[SMEM] + [VMEM] * 5,
        out_specs=(VMEM,) * 3,
        scratch_shapes=[
            pltpu.VMEM((HEADS, LEN, DH), F32),
            pltpu.VMEM((HEADS, LEN, DH), F32),
            pltpu.VMEM((128, D), F32),
        ],
        compiler_params=PARAMS,
        cost_estimate=pl.CostEstimate(
            flops=10 * HEADS * LEN * LEN * 256, bytes_accessed=LEN * HW * 14, transcendentals=0
        ),
        name="attend_back",
    )(info, qkv, grads, tokens, row_sums, bias_sums)


HBM = pl.BlockSpec(memory_space=pltpu.HBM)
WIDE = pltpu.CompilerParams(vmem_limit_bytes=60 * 1024 * 1024)


def pack(context_weight, expand_weight, reduce_weight):
    operands = (context_weight, expand_weight, reduce_weight, jnp.asarray(reorder_matrix(), BF16))
    return pl.pallas_call(
        pack_kernel,
        out_shape=jax.ShapeDtypeStruct((24, PACKED), BF16),
        in_specs=[HBM] * len(operands),
        out_specs=VMEM,
        scratch_shapes=[pltpu.VMEM(operand.shape, BF16) for operand in operands]
        + [pltpu.SemaphoreType.DMA((len(operands),))],
        compiler_params=WIDE,
        name="pack",
    )(*operands)


def early_pack(info, after, qkv_weight, vectors):
    operands = (qkv_weight, *vectors)
    return pl.pallas_call(
        early_kernel,
        out_shape=jax.ShapeDtypeStruct((32, 32, 3 * HW), BF16),
        in_specs=[SMEM] + [HBM] * (1 + len(operands)),
        out_specs=VMEM,
        scratch_shapes=[pltpu.VMEM(operand.shape, BF16) for operand in operands]
        + [pltpu.VMEM((8, 3 * HW), F32), pltpu.SemaphoreType.DMA((len(operands),))],
        compiler_params=WIDE,
        name="early_pack",
    )(info, after, *operands)


def finish_reduce_kernel(a_ref, b_ref, c_ref, d_ref, reduce_ref):
    for part in range(4):
        cols = slice(part * D, (part + 1) * D)
        parts = [ref[:, cols].astype(F32) for ref in (a_ref, b_ref, c_ref, d_ref)]
        reduce_ref[part * 24 : (part + 1) * 24, :] = (parts[0] + parts[1]) + (parts[2] + parts[3])


def finish_kernel(a_ref, b_ref, c_ref, d_ref, order_ref, expand_ref, context_ref):
    def total(start, width):
        parts = [ref[:, start : start + width].astype(F32) for ref in (a_ref, b_ref, c_ref, d_ref)]
        return (parts[0] + parts[1]) + (parts[2] + parts[3])

    context_ref[...] = total(FF, D)
    moved = [total(part * D, D) for part in range(4)]
    left = jnp.concatenate(
        [
            jnp.concatenate([values[:, q * HW : (q + 1) * HW] for values in moved], axis=1)
            for q in range(4)
        ],
        axis=0,
    )
    terms = []
    for _ in range(3):
        terms.append(left.astype(BF16))
        left = left - terms[-1].astype(F32)
    result = by_transpose(jnp.concatenate(terms, axis=0), order_ref[...])
    result = (result[:96] + result[96:192]) + result[192:]
    for q in range(4):
        expand_ref[:, q * D : (q + 1) * D] = result[q * 24 : (q + 1) * 24]


def finish_reduce(pieces):
    return pl.pallas_call(
        finish_reduce_kernel,
        out_shape=jax.ShapeDtypeStruct((96, D), F32),
        in_specs=[VMEM] * 4,
        out_specs=VMEM,
        compiler_params=PARAMS,
        name="finish_reduce",
    )(*pieces)


def finish(pieces):
    return pl.pallas_call(
        finish_kernel,
        out_shape=(
            jax.ShapeDtypeStruct((24, FF), F32),
            jax.ShapeDtypeStruct((24, D), F32),
        ),
        in_specs=[VMEM] * 5,
        out_specs=(VMEM,) * 2,
        compiler_params=PARAMS,
        name="finish",
    )(*pieces, jnp.asarray(reorder_matrix(), BF16))


def middle(info, context_tok, own, cotangent, rows, bias, weights):
    tall = (LOCAL, D)
    return pl.pallas_call(
        middle_kernel,
        out_shape=(
            jax.ShapeDtypeStruct(tall, BF16),
            jax.ShapeDtypeStruct(tall, F32),
            jax.ShapeDtypeStruct((SP, LOCAL, HW), BF16),
            jax.ShapeDtypeStruct((8, D), F32),
            jax.ShapeDtypeStruct((4, D), F32),
            jax.ShapeDtypeStruct((D, PACKED), BF16),
        ),
        in_specs=[SMEM] + [VMEM] * 5 + [pl.BlockSpec(memory_space=pl.ANY)],
        out_specs=(VMEM,) * 5 + (pl.BlockSpec(memory_space=pl.ANY),),
        scratch_shapes=[
            pltpu.VMEM((D, PACKED), BF16),
            pltpu.VMEM((D, PACKED), BF16),
            pltpu.VMEM((LOCAL, FF), F32),
            pltpu.VMEM((LOCAL, FF), BF16),
            pltpu.SemaphoreType.DMA((9,)),
            pltpu.SemaphoreType.DMA((9,)),
        ],
        compiler_params=pltpu.CompilerParams(vmem_limit_bytes=48 * 1024 * 1024),
        cost_estimate=pl.CostEstimate(
            flops=6 * LOCAL * D * PACKED, bytes_accessed=24 * 1024 * 1024, transcendentals=0
        ),
        name="middle",
    )(info, context_tok, own, cotangent, rows, bias, weights)


def from_x(values, x_at):
    pieces = [values] + [to_x(values, -step) for step in (1, 2, 3)]
    return rolled(jnp.stack(pieces), SP - x_at)


def per_device(
    hidden_in,
    lengths,
    qkv_weight,
    query_bias,
    value_bias,
    context_weight,
    context_bias,
    first_gain,
    first_shift,
    expand_weight,
    expand_bias,
    reduce_weight,
    reduce_bias,
    second_gain,
    second_shift,
    out_grad,
):
    x_at = lax.axis_index("sp")
    own = hidden_in[0]
    tokens = [own] + [None] * 3
    for step in ORDER:
        tokens[step] = to_x(own, -step)

    core = lax.axis_index("fsdp") & 1
    info = jnp.stack([x_at.astype(jnp.int32), lengths[0], core.astype(jnp.int32)])
    packed = pack(context_weight, expand_weight, reduce_weight)
    early = early_pack(
        info, packed, qkv_weight,
        (query_bias, value_bias, context_bias, first_gain, first_shift, reduce_bias,
         second_gain, second_shift, expand_bias),
    )
    packed = lax.all_gather(packed, "fsdp", axis=0, tiled=True)
    early = lax.all_to_all(early, "fsdp", split_axis=0, concat_axis=0, tiled=True)
    qkv_full = early[:, :24].reshape(D, 3 * HW)
    rows = jnp.swapaxes(early[:, 24:, :24], 0, 1).reshape(8, D).astype(F32)
    query_full, value_full = rows[0], rows[1]
    expand_add = jnp.swapaxes(early[:, 24, 128:224].reshape(32, 4, 24), 0, 1)
    expand_add = expand_add.reshape(1, FF).astype(F32)

    everyone = jnp.concatenate(tokens, axis=0)
    offsets = jnp.concatenate(
        [
            lax.dynamic_slice_in_dim(query_full, x_at * HW, HW),
            jnp.zeros((HW,), F32),
            lax.dynamic_slice_in_dim(value_full, x_at * HW, HW),
        ]
    )
    qkv = (dot(everyone, qkv_full) + offsets).astype(BF16)
    context = attend(info, qkv)

    groups = [context[:LOCAL]] + [None] * 3
    for step in ORDER:
        groups[SP - step] = to_x(context[step * LOCAL : (step + 1) * LOCAL], step)
    context_tok = jnp.stack(groups)

    hidden_out, grad_one, context_grad, row_sums, bias_sums, packed_grads = middle(
        info, context_tok, own, out_grad[0], rows, expand_add, packed
    )
    packed_grads = lax.psum_scatter(
        packed_grads,
        "fsdp",
        scatter_dimension=0,
        axis_index_groups=[[8 * z + m for m in range(8)] for z in range(4)],
        tiled=True,
    )
    z_at = lax.axis_index("fsdp") // 8

    def spread(start, width):
        rows = [
            lax.dynamic_slice(packed_grads, ((z_at + step) % 4 * 24, start), (24, width))
            for step in range(4)
        ]
        total = rows[0].astype(F32)
        for step in ORDER:
            total = total + to_z(rows[step], step).astype(F32)
        total = total.astype(BF16)
        return [total] + [to_x(total, step) for step in ORDER]

    reduce_parts = spread(0, FF)
    other_parts = spread(FF, FF + D)
    blocks = [context_grad[0]] + [None] * 3
    for step in ORDER:
        blocks[SP - step] = to_x(context_grad[step], step)
    grad_heads = jnp.concatenate(blocks, axis=0)

    qkv_grad, mine, other = attend_back(info, qkv, grad_heads, everyone, row_sums, bias_sums)
    second_round = (mine.astype(F32) + to_core(other).astype(F32)).astype(BF16)

    partial = by_transpose(qkv_grad, qkv_full).astype(BF16)
    input_sum = grad_one + partial[:LOCAL].astype(F32)
    for step in ORDER:
        input_sum = input_sum + to_x(partial[step * LOCAL : (step + 1) * LOCAL], step).astype(F32)
    input_grad = input_sum.astype(BF16)[None]

    second_round = lax.all_to_all(
        second_round.reshape(16, 24, LATE),
        "fsdp",
        split_axis=0,
        concat_axis=0,
        axis_index_groups=[[2 * chip + at for chip in range(16)] for at in range(2)],
        tiled=True,
    )
    second_round = jnp.sum(second_round.astype(F32), axis=0).astype(BF16)
    second_round = from_x(second_round, x_at).astype(F32)
    qkv_out = jnp.transpose(second_round[:, :, 128 : 128 + 3 * HW].reshape(SP, 24, 3, HW), (1, 2, 0, 3))
    qkv_out = qkv_out.reshape(24, 3 * D)
    eight = jnp.sum(second_round[:, :, :12], axis=0).T
    expand_bias_out = eight[8:].reshape(96)

    reduce_out = finish_reduce(reduce_parts)
    expand_out, context_out = finish(other_parts)

    return (
        hidden_out[None],
        input_grad,
        qkv_out,
        eight[0],
        eight[1],
        context_out,
        eight[2],
        eight[3],
        eight[4],
        expand_out,
        expand_bias_out,
        reduce_out,
        eight[5],
        eight[6],
        eight[7],
    )


def solution(mesh):
    sequences = P("fsdp", "sp", None)
    matrix = P("fsdp", None)
    vector = P("fsdp")
    return jax.shard_map(
        per_device,
        mesh=mesh,
        in_specs=(
            sequences, vector, matrix, vector, vector, matrix, vector, vector, vector,
            matrix, vector, matrix, vector, vector, vector, sequences,
        ),
        out_specs=(
            sequences, sequences, matrix, vector, vector, matrix, vector, vector, vector,
            matrix, vector, matrix, vector, vector, vector,
        ),
        check_vma=False,
    )
```

```python
import jax
import jax.numpy as jnp
import numpy as np
from jax import lax
from jax.experimental import pallas as pl
from jax.experimental.pallas import tpu as pltpu
from jax.sharding import PartitionSpec as P

D = 768
H = 12
DH = 64
FF = 3072
SP = 4
LOCAL = 256
LEN = 1024
HEADS = H // SP
HW = HEADS * DH
BLOCK = 256

EPSILON = 1e-06
SCALING = 0.125
MASKED = -1000000000.0
F32 = jnp.float32
BF16 = jnp.bfloat16


def normalize(values, gain_row, shift_row):
    average = jnp.mean(values, axis=-1, keepdims=True)
    centred = values - average
    inv_std = lax.rsqrt(jnp.mean(centred * centred, axis=-1, keepdims=True) + EPSILON)
    normed = centred * inv_std
    return (normed * gain_row + shift_row, normed, inv_std)


def normalize_back(upstream, normed, inv_std, gain_row):
    weighted = upstream * gain_row
    return inv_std * (
        weighted
        - jnp.mean(weighted, axis=-1, keepdims=True)
        - normed * jnp.mean(weighted * normed, axis=-1, keepdims=True)
    )


def dot(left_side, right_side):
    return jnp.dot(left_side, right_side, preferred_element_type=F32)


def rows_first(left_side, right_side):
    return lax.dot_general(
        left_side, right_side, (((0,), (0,)), ((), ())), preferred_element_type=F32
    )


def by_transpose(left_side, right_side):
    return lax.dot_general(
        left_side, right_side, (((1,), (1,)), ((), ())), preferred_element_type=F32
    )


ROOT = 0.7978845608028654
CUBE = 0.044715


def gate_and_slope(values):
    square = values * values
    bent = jnp.tanh(ROOT * values * (1.0 + CUBE * square))
    half = 0.5 * (1.0 + bent)
    slope = half + 0.5 * values * (1.0 - bent * bent) * (ROOT * (1.0 + 3.0 * CUBE * square))
    return values * half, slope


def to_x(values, step):
    return lax.ppermute(values, "sp", [(i, (i + step) % SP) for i in range(SP)])


def to_core(values):
    return lax.ppermute(values, "fsdp", [(i, i ^ 1) for i in range(32)])


def to_z(values, step):
    return lax.ppermute(values, "fsdp", [(i, (i + 8 * step) % 32) for i in range(32)])


ORDER = (1, 3, 2)


def rolled(values, start):
    count = values.shape[0]
    return lax.dynamic_slice_in_dim(
        jnp.concatenate([values, values], axis=0), start % count, count, axis=0
    )


def masked_keys(info_ref, shape, dim):
    at = lax.broadcasted_iota(jnp.int32, shape, dim)
    block = (info_ref[0] + lax.shift_right_logical(at, 8)) & 3
    return (block * LOCAL + (at & (LOCAL - 1))) < info_ref[1]


def attend_kernel(info_ref, qkv_ref, context_ref):
    valid = masked_keys(info_ref, (1, LEN), 1)

    @pl.loop(0, LEN // BLOCK)
    def _(step):
        rows = pl.ds(pl.multiple_of(step * BLOCK, BLOCK), BLOCK)
        outs = []
        for head in range(HEADS):
            cols = head * DH
            keys = qkv_ref[:, HW + cols : HW + cols + DH]
            vals = qkv_ref[:, 2 * HW + cols : 2 * HW + cols + DH]
            queries = qkv_ref[rows, cols : cols + DH] * jnp.asarray(SCALING, BF16)
            scores = jnp.where(valid, by_transpose(queries, keys), MASKED)
            weights = jnp.exp(scores - jnp.max(scores, axis=-1, keepdims=True))
            totals = jnp.sum(weights, axis=-1, keepdims=True)
            outs.append(dot(weights.astype(BF16), vals) * (1.0 / totals))
        context_ref[rows, :] = jnp.concatenate(outs, axis=1).astype(BF16)


def attend_back_kernel(
    info_ref, qkv_ref, grad_ref, tokens_ref, sums_ref, bias_sum_ref,
    out_ref, mine_ref, other_ref, key_sum, value_sum, stack,
):
    valid = masked_keys(info_ref, (LEN, 1), 0)
    key_sum[...] = jnp.zeros_like(key_sum)
    value_sum[...] = jnp.zeros_like(value_sum)

    @pl.loop(0, LEN // BLOCK)
    def _(step):
        rows = pl.ds(pl.multiple_of(step * BLOCK, BLOCK), BLOCK)
        outs = []
        for head in range(HEADS):
            cols = head * DH
            keys = qkv_ref[:, HW + cols : HW + cols + DH]
            vals = qkv_ref[:, 2 * HW + cols : 2 * HW + cols + DH]
            queries = qkv_ref[rows, cols : cols + DH] * jnp.asarray(SCALING, BF16)
            grads = grad_ref[rows, cols : cols + DH]
            scores = jnp.where(valid, by_transpose(keys, queries), MASKED)
            weights = jnp.exp(scores - jnp.max(scores, axis=0, keepdims=True))
            probs = weights * (1.0 / jnp.sum(weights, axis=0, keepdims=True))
            value_sum[head] += dot(probs.astype(BF16), grads)
            prob_grad = by_transpose(vals, grads)
            centre = jnp.sum(probs * prob_grad, axis=0, keepdims=True)
            score_grad = (probs * (prob_grad - centre)).astype(BF16)
            key_sum[head] += dot(score_grad, queries)
            outs.append(rows_first(score_grad, keys) * SCALING)
        out_ref[rows, :HW] = jnp.concatenate(outs, axis=1).astype(BF16)

    for part, total in ((1, key_sum), (2, value_sum)):
        out_ref[:, part * HW : (part + 1) * HW] = jnp.concatenate(
            [total[head] for head in range(HEADS)], axis=1
        ).astype(BF16)

    low = out_ref[...]
    sums = jnp.sum(low.astype(F32), axis=0, keepdims=True)
    stack[...] = jnp.zeros_like(stack)
    for row, part in ((0, 0), (1, 2)):
        own = sums[:, part * HW : (part + 1) * HW]
        stack[row : row + 1, :] = jnp.concatenate(
            [jnp.where(info_ref[0] == at, own, 0.0) for at in range(SP)], axis=1
        )
    stack[2:8, :] = sums_ref[0:6, :]
    stack[8:12, :] = bias_sum_ref[...]
    mine_ref[:, 128 + 3 * HW :] = jnp.zeros((D // 2, LATE - 128 - 3 * HW), BF16)
    other_ref[:, 128 + 3 * HW :] = jnp.zeros((D // 2, LATE - 128 - 3 * HW), BF16)
    for cols, full in (
        (slice(0, 128), stack[...].T),
        (slice(128, 128 + 3 * HW), rows_first(tokens_ref[...], low)),
    ):
        even, odd = (
            jnp.concatenate(
                [full[(2 * chip + at) * 24 : (2 * chip + at + 1) * 24] for chip in range(16)], axis=0
            )
            for at in range(2)
        )
        first = info_ref[2] == 0
        mine_ref[:, cols] = jnp.where(first, even, odd).astype(BF16)
        other_ref[:, cols] = jnp.where(first, odd, even).astype(BF16)


PACKED = 2 * FF + D
LATE = D


def reorder_matrix():
    source = np.arange(D).reshape(8, 4, 24).transpose(1, 0, 2).reshape(D)
    matrix = np.zeros((D, D), np.float32)
    matrix[source, np.arange(D)] = 1.0
    return matrix


def fetch(sources, held, sems):
    copies = [
        pltpu.make_async_copy(source, target, sems.at[at])
        for at, (source, target) in enumerate(zip(sources, held))
    ]
    for copy in copies:
        copy.start()
    for copy in copies:
        copy.wait()


def pack_kernel(*refs):
    packed_ref, held, sems = refs[4], refs[5:9], refs[9]
    fetch(refs[:4], held, sems)
    context_ref, expand_ref, reduce_ref, order_ref = held
    reduce_rows = reduce_ref[...].astype(F32)
    for part in range(4):
        packed_ref[:, part * D : (part + 1) * D] = reduce_rows[part * 24 : (part + 1) * 24].astype(BF16)
    stacked = jnp.concatenate(
        [expand_ref[:, q * D : (q + 1) * D].astype(F32) for q in range(4)], axis=0
    )
    stacked = dot(stacked.astype(BF16), order_ref[...])
    moved = [stacked[q * 24 : (q + 1) * 24] for q in range(4)]
    for part in range(4):
        packed_ref[:, FF + part * D : FF + (part + 1) * D] = jnp.concatenate(
            [values[:, part * HW : (part + 1) * HW] for values in moved], axis=1
        ).astype(BF16)
    packed_ref[:, 2 * FF :] = context_ref[...]


def early_kernel(info_ref, after_ref, *refs):
    early_ref, held, (rows_ref, sems) = refs[10], refs[11:21], refs[21:]
    fetch(refs[:10], held, sems)
    qkv_ref, vector_refs = held[0], held[1:]
    rows_ref[...] = jnp.zeros_like(rows_ref)
    for row in range(8):
        rows_ref[row : row + 1, :24] = vector_refs[row][...].astype(F32).reshape(1, 24)
    rows_ref[0:1, 128:224] = vector_refs[8][...].astype(F32).reshape(1, 96)
    for at in range(SP):

        @pl.when(info_ref[0] == at)
        def _(at=at):
            own = jnp.concatenate(
                [qkv_ref[:, part * D + at * HW : part * D + (at + 1) * HW] for part in range(3)],
                axis=1,
            )
            block = jnp.concatenate([own.astype(F32), rows_ref[...]], axis=0).astype(BF16)

            @pl.loop(0, 32)
            def _(owner):
                early_ref[owner] = block


def middle_kernel(
    info_ref, context_ref, own_ref, cotangent_ref, rows_ref, bias_ref, weights_ref,
    hidden_ref, grad_one_ref, context_grad_ref, sums_ref, bias_sum_ref, grads_ref,
    held, made, slopes, active, in_sems, out_sems,
):
    def piece(block):
        return slice(block * D, (block + 1) * D)

    copies = {}
    for block in (8, 4, 0, 5, 1, 6, 2, 7, 3):
        copies[block] = pltpu.make_async_copy(
            weights_ref.at[:, piece(block)], held.at[:, piece(block)], in_sems.at[block]
        )
        copies[block].start()

    def send(block):
        copy = pltpu.make_async_copy(
            made.at[:, piece(block)], grads_ref.at[:, piece(block)], out_sems.at[block]
        )
        copy.start()
        return copy

    context_add, gain_one, shift_one, reduce_add, gain_two, shift_two = (
        rows_ref[row : row + 1, :] for row in range(2, 8)
    )
    groups = [(z - info_ref[0]) & 3 for z in range(SP)]

    def by_plane(values):
        return jnp.concatenate(
            [values[(8 * z + m) * 24 : (8 * z + m + 1) * 24] for m in range(8) for z in range(4)],
            axis=0,
        ).astype(BF16)

    own = own_ref[...].astype(F32) + context_add
    copies[8].wait()
    for block in range(SP):
        own = own + dot(
            context_ref[groups[block]], held[block * HW : (block + 1) * HW, piece(8)]
        )
    first_out, normed_one, inv_one = normalize(own, gain_one, shift_one)
    first_low = first_out.astype(BF16)
    second_in = first_out + reduce_add
    for part in range(4):
        copies[4 + part].wait()
        expand = dot(first_low, held[:, piece(4 + part)]) + bias_ref[:, piece(part)]
        value, slope = gate_and_slope(expand)
        active[:, piece(part)] = value.astype(BF16)
        slopes[:, piece(part)] = slope
        copies[part].wait()
        second_in = second_in + dot(active[:, piece(part)], held[:, piece(part)])
    second_out, normed_two, inv_two = normalize(second_in, gain_two, shift_two)
    hidden_ref[...] = second_out.astype(BF16)

    cotangent = cotangent_ref[...].astype(F32)
    grad_two = normalize_back(cotangent, normed_two, inv_two, gain_two)
    reduced_grad = grad_two.astype(BF16)
    sums_ref[...] = jnp.zeros_like(sums_ref)
    sums_ref[3:4, :] = jnp.sum(reduced_grad.astype(F32), axis=0, keepdims=True)
    sums_ref[4:5, :] = jnp.sum(cotangent * normed_two, axis=0, keepdims=True)
    sums_ref[5:6, :] = jnp.sum(cotangent, axis=0, keepdims=True)
    first_grad = grad_two
    sent = []
    for part in range(4):
        active_grad = by_transpose(reduced_grad, held[:, piece(part)]).astype(BF16)
        expand_grad = (active_grad.astype(F32) * slopes[:, piece(part)]).astype(BF16)
        bias_sum_ref[part : part + 1, :] = jnp.sum(expand_grad.astype(F32), axis=0, keepdims=True)
        first_grad = first_grad + by_transpose(expand_grad, held[:, piece(4 + part)])
        made[:, piece(part)] = by_plane(rows_first(active[:, piece(part)], reduced_grad))
        sent.append(send(part))
        made[:, piece(4 + part)] = by_plane(rows_first(first_low, expand_grad))
        sent.append(send(4 + part))
    sums_ref[1:2, :] = jnp.sum(first_grad * normed_one, axis=0, keepdims=True)
    sums_ref[2:3, :] = jnp.sum(first_grad, axis=0, keepdims=True)
    grad_one = normalize_back(first_grad, normed_one, inv_one, gain_one)
    grad_one_ref[...] = grad_one
    branch_grad = grad_one.astype(BF16)
    sums_ref[0:1, :] = jnp.sum(branch_grad.astype(F32), axis=0, keepdims=True)
    made[:, piece(8)] = by_plane(
        jnp.concatenate([rows_first(context_ref[group], branch_grad) for group in groups], axis=0)
    )
    sent.append(send(8))
    for block in range(SP):
        context_grad_ref[groups[block]] = by_transpose(
            branch_grad, held[block * HW : (block + 1) * HW, piece(8)]
        ).astype(BF16)
    for copy in sent:
        copy.wait()


SMEM = pl.BlockSpec(memory_space=pltpu.SMEM)
VMEM = pl.BlockSpec(memory_space=pltpu.VMEM)
PARAMS = pltpu.CompilerParams(vmem_limit_bytes=40 * 1024 * 1024)


def attend(info, qkv):
    return pl.pallas_call(
        attend_kernel,
        out_shape=jax.ShapeDtypeStruct((LEN, HW), BF16),
        in_specs=[SMEM, VMEM],
        out_specs=VMEM,
        compiler_params=PARAMS,
        cost_estimate=pl.CostEstimate(
            flops=4 * HEADS * LEN * LEN * 256, bytes_accessed=LEN * HW * 8, transcendentals=0
        ),
        name="attend",
    )(info, qkv)


def attend_back(info, qkv, grads, tokens, row_sums, bias_sums):
    return pl.pallas_call(
        attend_back_kernel,
        out_shape=(
            jax.ShapeDtypeStruct((LEN, 3 * HW), BF16),
            jax.ShapeDtypeStruct((D // 2, LATE), BF16),
            jax.ShapeDtypeStruct((D // 2, LATE), BF16),
        ),
        in_specs=[SMEM] + [VMEM] * 5,
        out_specs=(VMEM,) * 3,
        scratch_shapes=[
            pltpu.VMEM((HEADS, LEN, DH), F32),
            pltpu.VMEM((HEADS, LEN, DH), F32),
            pltpu.VMEM((128, D), F32),
        ],
        compiler_params=PARAMS,
        cost_estimate=pl.CostEstimate(
            flops=10 * HEADS * LEN * LEN * 256, bytes_accessed=LEN * HW * 14, transcendentals=0
        ),
        name="attend_back",
    )(info, qkv, grads, tokens, row_sums, bias_sums)


HBM = pl.BlockSpec(memory_space=pltpu.HBM)
WIDE = pltpu.CompilerParams(vmem_limit_bytes=60 * 1024 * 1024)


def pack(context_weight, expand_weight, reduce_weight):
    operands = (context_weight, expand_weight, reduce_weight, jnp.asarray(reorder_matrix(), BF16))
    return pl.pallas_call(
        pack_kernel,
        out_shape=jax.ShapeDtypeStruct((24, PACKED), BF16),
        in_specs=[HBM] * len(operands),
        out_specs=VMEM,
        scratch_shapes=[pltpu.VMEM(operand.shape, BF16) for operand in operands]
        + [pltpu.SemaphoreType.DMA((len(operands),))],
        compiler_params=WIDE,
        name="pack",
    )(*operands)


def early_pack(info, after, qkv_weight, vectors):
    operands = (qkv_weight, *vectors)
    return pl.pallas_call(
        early_kernel,
        out_shape=jax.ShapeDtypeStruct((32, 32, 3 * HW), BF16),
        in_specs=[SMEM] + [HBM] * (1 + len(operands)),
        out_specs=VMEM,
        scratch_shapes=[pltpu.VMEM(operand.shape, BF16) for operand in operands]
        + [pltpu.VMEM((8, 3 * HW), F32), pltpu.SemaphoreType.DMA((len(operands),))],
        compiler_params=WIDE,
        name="early_pack",
    )(info, after, *operands)


def finish_reduce_kernel(a_ref, b_ref, c_ref, d_ref, reduce_ref):
    for part in range(4):
        cols = slice(part * D, (part + 1) * D)
        parts = [ref[:, cols].astype(F32) for ref in (a_ref, b_ref, c_ref, d_ref)]
        reduce_ref[part * 24 : (part + 1) * 24, :] = (parts[0] + parts[1]) + (parts[2] + parts[3])


def finish_kernel(a_ref, b_ref, c_ref, d_ref, order_ref, expand_ref, context_ref):
    def total(start, width):
        parts = [ref[:, start : start + width].astype(F32) for ref in (a_ref, b_ref, c_ref, d_ref)]
        return (parts[0] + parts[1]) + (parts[2] + parts[3])

    context_ref[...] = total(FF, D)
    moved = [total(part * D, D) for part in range(4)]
    left = jnp.concatenate(
        [
            jnp.concatenate([values[:, q * HW : (q + 1) * HW] for values in moved], axis=1)
            for q in range(4)
        ],
        axis=0,
    )
    terms = []
    for _ in range(3):
        terms.append(left.astype(BF16))
        left = left - terms[-1].astype(F32)
    result = by_transpose(jnp.concatenate(terms, axis=0), order_ref[...])
    result = (result[:96] + result[96:192]) + result[192:]
    for q in range(4):
        expand_ref[:, q * D : (q + 1) * D] = result[q * 24 : (q + 1) * 24]


def finish_reduce(pieces):
    return pl.pallas_call(
        finish_reduce_kernel,
        out_shape=jax.ShapeDtypeStruct((96, D), F32),
        in_specs=[VMEM] * 4,
        out_specs=VMEM,
        compiler_params=PARAMS,
        name="finish_reduce",
    )(*pieces)


def finish(pieces):
    return pl.pallas_call(
        finish_kernel,
        out_shape=(
            jax.ShapeDtypeStruct((24, FF), F32),
            jax.ShapeDtypeStruct((24, D), F32),
        ),
        in_specs=[VMEM] * 5,
        out_specs=(VMEM,) * 2,
        compiler_params=PARAMS,
        name="finish",
    )(*pieces, jnp.asarray(reorder_matrix(), BF16))


def middle(info, context_tok, own, cotangent, rows, bias, weights):
    tall = (LOCAL, D)
    return pl.pallas_call(
        middle_kernel,
        out_shape=(
            jax.ShapeDtypeStruct(tall, BF16),
            jax.ShapeDtypeStruct(tall, F32),
            jax.ShapeDtypeStruct((SP, LOCAL, HW), BF16),
            jax.ShapeDtypeStruct((8, D), F32),
            jax.ShapeDtypeStruct((4, D), F32),
            jax.ShapeDtypeStruct((D, PACKED), BF16),
        ),
        in_specs=[SMEM] + [VMEM] * 5 + [pl.BlockSpec(memory_space=pl.ANY)],
        out_specs=(VMEM,) * 5 + (pl.BlockSpec(memory_space=pl.ANY),),
        scratch_shapes=[
            pltpu.VMEM((D, PACKED), BF16),
            pltpu.VMEM((D, PACKED), BF16),
            pltpu.VMEM((LOCAL, FF), F32),
            pltpu.VMEM((LOCAL, FF), BF16),
            pltpu.SemaphoreType.DMA((9,)),
            pltpu.SemaphoreType.DMA((9,)),
        ],
        compiler_params=pltpu.CompilerParams(vmem_limit_bytes=48 * 1024 * 1024),
        cost_estimate=pl.CostEstimate(
            flops=6 * LOCAL * D * PACKED, bytes_accessed=24 * 1024 * 1024, transcendentals=0
        ),
        name="middle",
    )(info, context_tok, own, cotangent, rows, bias, weights)


def from_x(values, x_at):
    pieces = [values] + [to_x(values, -step) for step in (1, 2, 3)]
    return rolled(jnp.stack(pieces), SP - x_at)


def per_device(
    hidden_in,
    lengths,
    qkv_weight,
    query_bias,
    value_bias,
    context_weight,
    context_bias,
    first_gain,
    first_shift,
    expand_weight,
    expand_bias,
    reduce_weight,
    reduce_bias,
    second_gain,
    second_shift,
    out_grad,
):
    x_at = lax.axis_index("sp")
    own = hidden_in[0]
    tokens = [own] + [None] * 3
    for step in ORDER:
        tokens[step] = to_x(own, -step)

    core = lax.axis_index("fsdp") & 1
    info = jnp.stack([x_at.astype(jnp.int32), lengths[0], core.astype(jnp.int32)])
    packed = pack(context_weight, expand_weight, reduce_weight)
    early = early_pack(
        info, packed, qkv_weight,
        (query_bias, value_bias, context_bias, first_gain, first_shift, reduce_bias,
         second_gain, second_shift, expand_bias),
    )
    packed = lax.all_gather(packed, "fsdp", axis=0, tiled=True)
    early = lax.all_to_all(early, "fsdp", split_axis=0, concat_axis=0, tiled=True)
    qkv_full = early[:, :24].reshape(D, 3 * HW)
    rows = jnp.swapaxes(early[:, 24:, :24], 0, 1).reshape(8, D).astype(F32)
    query_full, value_full = rows[0], rows[1]
    expand_add = jnp.swapaxes(early[:, 24, 128:224].reshape(32, 4, 24), 0, 1)
    expand_add = expand_add.reshape(1, FF).astype(F32)

    everyone = jnp.concatenate(tokens, axis=0)
    offsets = jnp.concatenate(
        [
            lax.dynamic_slice_in_dim(query_full, x_at * HW, HW),
            jnp.zeros((HW,), F32),
            lax.dynamic_slice_in_dim(value_full, x_at * HW, HW),
        ]
    )
    qkv = (dot(everyone, qkv_full) + offsets).astype(BF16)
    context = attend(info, qkv)

    groups = [context[:LOCAL]] + [None] * 3
    for step in ORDER:
        groups[SP - step] = to_x(context[step * LOCAL : (step + 1) * LOCAL], step)
    context_tok = jnp.stack(groups)

    hidden_out, grad_one, context_grad, row_sums, bias_sums, packed_grads = middle(
        info, context_tok, own, out_grad[0], rows, expand_add, packed
    )
    packed_grads = lax.psum_scatter(
        packed_grads,
        "fsdp",
        scatter_dimension=0,
        axis_index_groups=[[8 * z + m for m in range(8)] for z in range(4)],
        tiled=True,
    )
    z_at = lax.axis_index("fsdp") // 8

    def spread(start, width):
        rows = [
            lax.dynamic_slice(packed_grads, ((z_at + step) % 4 * 24, start), (24, width))
            for step in range(4)
        ]
        total = rows[0].astype(F32)
        for step in (2, 1, 3):
            total = total + to_z(rows[step], step).astype(F32)
        total = total.astype(BF16)
        return [total] + [to_x(total, step) for step in (2, 1, 3)]

    reduce_parts = spread(0, FF)
    other_parts = spread(FF, FF + D)
    blocks = [context_grad[0]] + [None] * 3
    for step in ORDER:
        blocks[SP - step] = to_x(context_grad[step], step)
    grad_heads = jnp.concatenate(blocks, axis=0)

    qkv_grad, mine, other = attend_back(info, qkv, grad_heads, everyone, row_sums, bias_sums)
    second_round = (mine.astype(F32) + to_core(other).astype(F32)).astype(BF16)

    partial = by_transpose(qkv_grad, qkv_full).astype(BF16)
    input_sum = grad_one + partial[:LOCAL].astype(F32)
    for step in ORDER:
        input_sum = input_sum + to_x(partial[step * LOCAL : (step + 1) * LOCAL], step).astype(F32)
    input_grad = input_sum.astype(BF16)[None]

    second_round = lax.all_to_all(
        second_round.reshape(16, 24, LATE),
        "fsdp",
        split_axis=0,
        concat_axis=0,
        axis_index_groups=[[2 * chip + at for chip in range(16)] for at in range(2)],
        tiled=True,
    )
    second_round = jnp.sum(second_round.astype(F32), axis=0).astype(BF16)
    second_round = from_x(second_round, x_at).astype(F32)
    qkv_out = jnp.transpose(second_round[:, :, 128 : 128 + 3 * HW].reshape(SP, 24, 3, HW), (1, 2, 0, 3))
    qkv_out = qkv_out.reshape(24, 3 * D)
    eight = jnp.sum(second_round[:, :, :12], axis=0).T
    expand_bias_out = eight[8:].reshape(96)

    reduce_out = finish_reduce(reduce_parts)
    expand_out, context_out = finish(other_parts)

    return (
        hidden_out[None],
        input_grad,
        qkv_out,
        eight[0],
        eight[1],
        context_out,
        eight[2],
        eight[3],
        eight[4],
        expand_out,
        expand_bias_out,
        reduce_out,
        eight[5],
        eight[6],
        eight[7],
    )


def solution(mesh):
    sequences = P("fsdp", "sp", None)
    matrix = P("fsdp", None)
    vector = P("fsdp")
    return jax.shard_map(
        per_device,
        mesh=mesh,
        in_specs=(
            sequences, vector, matrix, vector, vector, matrix, vector, vector, vector,
            matrix, vector, matrix, vector, vector, vector, sequences,
        ),
        out_specs=(
            sequences, sequences, matrix, vector, vector, matrix, vector, vector, vector,
            matrix, vector, matrix, vector, vector, vector,
        ),
        check_vma=False,
    )
```
